256 devices in a mesh: leaf: 64 (over z, y, core), sub: 4 (over x).
Axes of the slice: x: 4, y: 4, z: 8, core: 2. Of those that a mesh axis runs over, the one named last changes fastest.
Arguments:
- coupling: float32 [524288, 4, 128], P(('leaf', 'sub')), may hold values from -40 to 40, as said below
- weights: float32 [524288], P(('leaf', 'sub')), may hold values from 0.3 to 3, as said below
- rhs: float32 [524288, 128], P(('leaf', 'sub')), may hold values from -6 to 6
- order: int32 [256, 2048], P(('leaf', 'sub')), may hold values from 0 to 2047, each once within a row
Outputs:
- applied: float32 [524288, 4, 128], P(('leaf', 'sub'))
- answer: float32 [524288, 128], P(('leaf', 'sub'))
The draws below stay inside these ranges and needn't reach their ends.
Inputs may be any that keep to these rules, and one draw needn't show every extreme that they name: coupling and weights are finite and bounded as stated. weights are positive. `order`: each row is a permutation of 0 to 2047.
All inputs are finite; a program needn't handle non-finite values.
Results may differ from the reference program's by a relative error of at most 0.00024.
Values sent between devices are 32-bit elements; how exact they have to be, the bound alone decides.
A program may use at most 128 MiB of HBM per device.

```python
import jax
import jax.numpy as jnp
from jax import lax

CAP = 128
LEVELS = 4
AG_DEV = 2048
AGENTS = 524288
N_LEAF = 64
N_SUB = 4


def draw_coupling(key, part):
    key = jax.random.fold_in(key, 11)
    key_feat, key_basis, key_jitter, key_scale = jax.random.split(key, 4)
    features = jnp.clip(jax.random.normal(key_feat, (AGENTS, 16), jnp.float32), -4.0, 4.0)
    basis_mix = jnp.clip(jax.random.normal(key_basis, (LEVELS, 16, CAP), jnp.float32), -4.0, 4.0) * 0.25
    common = jnp.einsum('af,lfc->alc', features, basis_mix, precision=lax.Precision.HIGHEST)
    jitter = jnp.clip(jax.random.normal(key_jitter, (AGENTS, LEVELS, CAP), jnp.float32), -4.0, 4.0)
    log_lo, log_hi = (jnp.log(0.4), jnp.log(4.0))
    row_scale = jnp.exp(jax.random.uniform(key_scale, (AGENTS, 1, 1), jnp.float32, log_lo, log_hi))
    return jnp.clip(row_scale * (common + jitter), -40.0, 40.0).astype(jnp.float32)


def draw_weights(key, part):
    key = jax.random.fold_in(key, 12)
    weight_base = jnp.exp(jax.random.uniform(key, (AGENTS,), jnp.float32, jnp.log(0.3), 0.0))
    position = jnp.arange(AGENTS, dtype=jnp.float32) / AGENTS
    return (weight_base * (1.0 + 2.0 * position)).astype(jnp.float32)


def levels(stream_key, dims, cuts, smallest, high):
    level = 1.0
    for dim, blocks in cuts:
        heights = jax.random.uniform(jax.random.fold_in(jax.random.fold_in(stream_key, 6), dim), (blocks,), jnp.float32, smallest / len(cuts), high / len(cuts))
        level = level * jnp.repeat(jnp.exp(heights), dims[dim] // blocks).reshape((-1,) + (1,) * (len(dims) - 1 - dim))
    return level


def noise(stream_key, dims, spread, most, cuts=(), kind=jnp.bfloat16):
    result = jax.random.normal(stream_key, dims, jnp.float32) * spread
    if len(cuts) > 0:
        result = levels(stream_key, dims, cuts, -0.22, 0.18) * result
    return jnp.clip(result, min=-most, max=most).astype(kind)


def setup_inputs(seed: int = 0) -> dict:
    seeds = jax.random.split(jax.random.key(seed), 5)
    return {
        "coupling": draw_coupling(jax.random.fold_in(seeds[4], 71), 0),
        "weights": draw_weights(jax.random.fold_in(seeds[4], 71), 0),
        "rhs": noise(seeds[2], (AGENTS, CAP), 1.0, 6.0, ((0, 256),), jnp.float32),
        "order": jax.vmap(lambda own: jax.random.permutation(own, AG_DEV))(jax.random.split(seeds[3], (N_LEAF * N_SUB))).reshape((N_LEAF * N_SUB, AG_DEV)).astype(jnp.int32),
    }


def capacitance(moments):
    width_cap = moments.shape[0]
    identity_mat = jnp.eye(width_cap, dtype=jnp.float32)
    system = identity_mat + moments[:, :width_cap]
    system = 0.5 * (system + system.T)
    factor = jnp.linalg.cholesky(system)
    forward = lax.linalg.triangular_solve(factor, moments[:, width_cap:], left_side=True, lower=True)
    return lax.linalg.triangular_solve(factor, forward, left_side=True, lower=True, transpose_a=True)

def reference(coupling, weights, rhs, order):
    block_start = (jnp.arange(order.shape[0], dtype=jnp.int32) * AG_DEV)[:, None]
    flat_index = (block_start + order).reshape(-1).astype(jnp.int32)
    coupling_rows = coupling[flat_index]
    weight_rows = weights[flat_index]
    source = rhs[flat_index]
    applied = weight_rows[:, None, None] * coupling_rows
    answer = weight_rows[:, None] * source
    for level_now in range(LEVELS - 1, -1, -1):
        node_count = 2 ** level_now
        node_rows = AGENTS // node_count
        lead_basis = applied[:, level_now, :].reshape(node_count, node_rows, CAP)
        pieces = [coupling_rows[:, level_now, :]] + [coupling_rows[:, coarse, :] for coarse in range(level_now)] + [source]
        columns = jnp.concatenate(pieces, axis=1).reshape(node_count, node_rows, -1)
        moments = jnp.einsum('nrc,nrd->ncd', lead_basis, columns, precision=lax.Precision.HIGHEST) / node_rows
        right_blocks = jax.vmap(capacitance)(moments)
        change = jnp.einsum('nrc,ncd->nrd', lead_basis, right_blocks, precision=lax.Precision.HIGHEST).reshape(AGENTS, -1)
        for coarse in range(level_now):
            applied = applied.at[:, coarse, :].add(-change[:, coarse * CAP:(coarse + 1) * CAP])
        answer = answer - change[:, level_now * CAP:]
    return (applied, answer)
```

```python
import jax
import jax.numpy as jnp
from jax import lax
from jax.experimental import pallas as pl
from jax.experimental.pallas import tpu as pltpu
from jax.sharding import PartitionSpec as P

MESH = pl.DeviceIdType.MESH
F32 = jnp.float32
BF = jnp.bfloat16
ROWS = 2048
CAP = 128
AGENTS = 524288
CHUNK = 256


def split(x):
    head = x.astype(BF)
    return head, (x - head.astype(F32)).astype(BF)


def dot3(a, b, contract=((1,), (0,))):
    def one(p, q):
        return lax.dot_general(p, q, (contract, ((), ())), preferred_element_type=F32)

    return one(a[0], b[0]) + (one(a[0], b[1]) + one(a[1], b[0]))


def dot_full(a, b):
    return jnp.dot(a, b, precision=lax.Precision.HIGHEST, preferred_element_type=F32)


def sub_bcast(v, i):
    return jnp.broadcast_to(v[i : i + 1, :], (8, 128))


def lane_bcast(v, j):
    return jnp.broadcast_to(v[:, j : j + 1], (8, 128))


def recip(x):
    r = pltpu.reciprocal(x, approx=True)
    return r * (2.0 - x * r)


def eliminate_panel(rows, off, lane, sub):
    cols = [lane_bcast(rows, off + j) for j in range(8)]
    out = jnp.where(
        (lane >= off) & (lane < off + 8), jnp.where(lane - off == sub, 1.0, 0.0), rows
    )
    for i in range(0, 8, 2):
        ci, cj = cols[i], cols[i + 1]
        a, b = sub_bcast(ci, i), sub_bcast(cj, i)
        b2, c = sub_bcast(ci, i + 1), sub_bcast(cj, i + 1)
        inv_det = recip(a * c - b * b2)
        n0 = jnp.where(sub == i, -c, jnp.where(sub == i + 1, b2, ci * c - cj * b2))
        n1 = jnp.where(sub == i, b, jnp.where(sub == i + 1, -a, cj * a - ci * b))
        f0, f1 = n0 * inv_det, n1 * inv_det
        keep = (sub != i) & (sub != i + 1)

        def update(v):
            return jnp.where(keep, v, 0.0) - f0 * sub_bcast(v, i) - f1 * sub_bcast(v, i + 1)

        for j in range(i + 2, 8):
            cols[j] = update(cols[j])
        out = update(out)
    return out


def rank8(v, cols, rows):
    t = [cols[j] * rows[j] for j in range(8)]
    return v - (((t[0] + t[1]) + (t[2] + t[3])) + ((t[4] + t[5]) + (t[6] + t[7])))


def invert(matrix, block=8):
    s = [matrix[8 * q : 8 * q + 8, :] for q in range(16)]
    lane = lax.broadcasted_iota(jnp.int32, (8, 128), 1)
    sub = lax.broadcasted_iota(jnp.int32, (8, 128), 0)
    for first in range(0, 16, block):
        for k in range(block):
            off = 8 * (first + k)
            inside = (lane >= off) & (lane < off + 8)
            u = eliminate_panel(s[first + k], off, lane, sub)
            us = [sub_bcast(u, j) for j in range(8)]
            for t in [(k + 1 + m) % block for m in range(block - 1)]:
                v = s[first + t]
                cols = [lane_bcast(v, off + j) for j in range(8)]
                s[first + t] = rank8(jnp.where(inside, 0.0, v), cols, us)
            s[first + k] = u
        rest = [(first + block + m) % 16 for m in range(16 - block)]
        left = jnp.concatenate([s[q] for q in rest], axis=0)
        left_lane = lax.broadcasted_iota(jnp.int32, left.shape, 1)
        inside = (left_lane >= 8 * first) & (left_lane < 8 * (first + block))
        parts = [jnp.zeros((8, 128), F32)] * 16
        parts[first : first + block] = s[first : first + block]
        wide = jnp.concatenate(parts, axis=0)
        new = jnp.where(inside, 0.0, left) - dot_full(jnp.where(inside, left, 0.0), wide)
        for m, q in enumerate(rest):
            s[q] = new[8 * m : 8 * m + 8]
    return jnp.concatenate(s, axis=0)


def kernel(
    order, w_s, w_v, coup_hbm, coup_rows_hbm, rhs_hbm, rhs_rows_hbm, applied, answer,
    coup, coup_rows, rhs, rhs_rows, in_sem, xh, xl, wh, wl,
    ga, ra, sa, rsa, pa, fa,
    gb, rb, sb, rsb, pb, fb,
    z1s, z1r, z1ps, z1pr, p2, fc,
    z2s, z2r, z2ps, z2pr, p1, fd,
    z4s, z4r,
    ph, plo, pt,
    core_sem, rsa_sem, aga_sem, rsb_sem, agb_sem, agc_sem, agd_sem, z_sem,
):
    leaf = lax.axis_index("leaf")
    x = lax.axis_index("sub")
    z, y, c = leaf // 8, (leaf // 2) % 4, leaf % 2
    me = x * 4 + y

    def device(px, py, pz, pc):
        return (pz * 8 + py * 2 + pc, px)

    plane = []
    for dx in range(4):
        for dy in range(4):
            if (dx, dy) != (0, 0):
                plane.append(((x + dx) % 4, (y + dy) % 4))
    core_id = device(x, y, z, 1 - c)
    plane_ids = [device(px, py, z, c) for px, py in plane]
    plane_q = [px * 4 + py for px, py in plane]
    cross_ids = [device(px, py, z, 1 - c) for px, py in plane]
    all_ids = plane_ids + cross_ids + [core_id]

    def z_flip(bit):
        return device(x, y, z + bit - 2 * bit * ((z // bit) % 2), c)

    z_ids = [z_flip(1), z_flip(2), z_flip(4)]

    quarter = ROWS // 4
    loads = []
    for i in range(4):
        at, at4 = pl.ds(quarter * i, quarter), pl.ds(4 * quarter * i, 4 * quarter)
        loads.append(pltpu.make_async_copy(coup_hbm.at[at4], coup.at[at4], in_sem.at[i]))
        loads.append(pltpu.make_async_copy(rhs_hbm.at[at], rhs.at[at], in_sem.at[4 + i]))
    rows_load = pltpu.make_async_copy(coup_rows_hbm, coup_rows, in_sem.at[8])
    for copy in loads:
        copy.start()
    rows_load.start()
    rhs_load = pltpu.make_async_copy(rhs_rows_hbm, rhs_rows, in_sem.at[9])
    rhs_load.start()

    barrier = pltpu.get_barrier_semaphore()
    for d in all_ids + z_ids:
        pl.semaphore_signal(barrier, inc=1, device_id=d, device_id_type=MESH)

    def send(src, dst, sems, i, d):
        copy = pltpu.make_async_remote_copy(
            src_ref=src, dst_ref=dst, send_sem=sems.at[0, i], recv_sem=sems.at[1, i],
            device_id=d, device_id_type=MESH,
        )
        copy.start()
        return copy

    def wait(copies):
        for copy in copies:
            copy.wait()

    weight_cols = jnp.concatenate([w_v[...], jnp.zeros((112, 128), F32)], axis=0).T
    for g in range(16):
        if g % 4 == 0:
            wait(loads[g // 2 : g // 2 + 2])
        r0 = 128 * g
        col = jnp.broadcast_to(weight_cols[:, g : g + 1], (128, 128))
        for k in range(4):
            j = 3 - k
            basis = coup[pl.ds(4 * r0 + k, 128, stride=4), :]
            h, l = split(basis)
            xh[r0 : r0 + 128, 128 * j : 128 * j + 128] = h
            xl[r0 : r0 + 128, 128 * j : 128 * j + 128] = l
            h, l = split(basis * col)
            wh[r0 : r0 + 128, 128 * j : 128 * j + 128] = h
            wl[r0 : r0 + 128, 128 * j : 128 * j + 128] = l
        h, l = split(rhs[r0 : r0 + 128, :])
        xh[r0 : r0 + 128, 512:640] = h
        xl[r0 : r0 + 128, 512:640] = l

    def gram(a0, a1, b0, b1):
        return dot3(
            (wh[:, a0:a1], wl[:, a0:a1]), (xh[:, b0:b1], xl[:, b0:b1]), ((0,), (0,))
        )

    def pieces(block):
        return block.reshape(16, 8, 128)

    m = gram(0, 128, 0, 256)
    ga[:, 0] = pieces(m[:, :128])
    ga[:, 1] = pieces(m[:, 128:])
    pl.semaphore_wait(barrier, len(all_ids) + 3)
    core_a = send(ga, ra, core_sem, 0, core_id)
    m = gram(0, 128, 256, 640)
    gb[0, :, 0] = pieces(m[:, :128])
    gb[0, :, 1] = pieces(m[:, 128:256])
    gb[1, :, 0] = pieces(m[:, 256:])
    core_a.wait()
    sa[...] = ga[...] + ra[...]
    rs_a = [send(sa.at[q], rsa.at[i], rsa_sem, i, d) for i, (q, d) in enumerate(zip(plane_q, plane_ids))]
    m = gram(128, 256, 128, 640)
    gb[1, :, 1] = pieces(m[:, :128])
    gb[0, :, 2] = pieces(m[:, 128:256])
    gb[0, :, 3] = pieces(m[:, 256:384])
    gb[1, :, 2] = pieces(m[:, 384:])
    m = gram(256, 512, 256, 640)
    gb[1, :, 3] = pieces(m[:128, :128])
    gb[0, :, 4] = pieces(m[:128, 128:256])
    gb[0, :, 5] = pieces(m[:128, 256:])
    gb[1, :, 4] = pieces(m[128:, 128:256])
    gb[1, :, 5] = pieces(m[128:, 256:])
    core_b = send(gb.at[1 - c], rb, core_sem, 1, core_id)
    wait(rs_a)
    pa[...] = sa[me] + jnp.sum(rsa[...], axis=0)
    fa[me] = pa[...]
    ag_a = [send(pa, fa.at[me], aga_sem, i, d) for i, d in enumerate(plane_ids)]
    core_b.wait()
    sb[...] = gb[c] + rb[...]
    rs_b = [send(sb.at[q], rsb.at[i], rsb_sem, i, d) for i, (q, d) in enumerate(zip(plane_q, plane_ids))]

    def permute(first, count):
        def body(t, carry):
            for u in range(8):
                i = first + t * 8 + u
                r = order[i]
                s = w_s[r]
                applied[pl.ds(pl.multiple_of(4 * i, 4), 4), :] = coup_rows[r] * s
                answer[pl.ds(i, 1), :] = rhs_rows[r] * s
            return carry

        lax.fori_loop(0, count // 8, body, 0)

    rows_load.wait()
    rhs_load.wait()
    permute(0, ROWS // 2)
    wait(rs_b)
    pb[...] = sb[me] + jnp.sum(rsb[...], axis=0)

    def gather_all(src, dst, sems):
        return [send(src, dst.at[c, me], sems, i, d) for i, d in enumerate(all_ids)]

    fb[c, me] = pb[0:2]
    ag_b = gather_all(pb.at[0:2], fb, agb_sem)
    permute(ROWS // 2, ROWS // 2)

    def block(ref, *at):
        return ref[at].reshape(128, 128)

    eye = jnp.where(
        lax.broadcasted_iota(jnp.int32, (128, 128), 0)
        == lax.broadcasted_iota(jnp.int32, (128, 128), 1),
        1.0,
        0.0,
    )

    def solve(lead, others, scale):
        inverse = invert(eye + lead * scale) * scale
        return inverse, others

    def subtract(level, columns):
        first = sum(128 * (k + 1) for k in range(3, level, -1))

        def body(t, carry):
            r0 = pl.multiple_of(t * CHUNK, CHUNK)
            lead = split(applied[pl.ds(4 * r0 + level, CHUNK, stride=4), :])
            change = dot3(
                lead,
                (ph[:, first : first + 128 * columns], plo[:, first : first + 128 * columns]),
            )
            for k in range(level):
                at = pl.ds(4 * r0 + level - 1 - k, CHUNK, stride=4)
                applied[at, :] = applied[at, :] - change[:, 128 * k : 128 * k + 128]
            at = pl.ds(r0, CHUNK)
            answer[at, :] = answer[at, :] - change[:, 128 * level :]
            return carry

        lax.fori_loop(0, ROWS // CHUNK, body, 0)

    def keep_p(level, p):
        first = sum(128 * (k + 1) for k in range(3, level, -1))
        h, l = split(p)
        ph[:, first : first + p.shape[1]] = h
        plo[:, first : first + p.shape[1]] = l

    pick = c == 0
    mine = pl.ds(pl.multiple_of(8 * me, 8), 8)

    wait(ag_a)
    scale = 8.0 / AGENTS
    inverse = invert(eye + block(fa, slice(None), 0) * scale) * scale
    wait(ag_b)
    m32 = block(fa, slice(None), 1)
    m3 = jnp.concatenate(
        [m32, block(fb, 0, slice(None), 0), block(fb, 0, slice(None), 1), block(fb, 1, slice(None), 0)],
        axis=1,
    )
    p3 = dot_full(inverse, m3)
    for k in range(3):
        pt[128 * k : 128 * k + 128, :] = p3[:, 128 * k : 128 * k + 128].T
    z1s[...] = block(fb, 1, slice(None), 1) - dot_full(pt[0:128, :], m32)
    z1 = [send(z1s, z1r, z_sem, 0, z_ids[0])]
    left = jnp.concatenate([pt[pl.ds(pl.multiple_of(128 * k + 8 * me, 8), 8), :] for k in range(3)], axis=0)
    part = dot_full(left, m3[:, 128:])
    z1ps[0] = pb[2] - jnp.where(pick, part[0:8, 0:128], part[0:8, 256:384])
    z1ps[1] = pb[3] - jnp.where(pick, part[0:8, 128:256], part[8:16, 0:128])
    z1ps[2] = pb[4] - jnp.where(pick, part[8:16, 128:256], part[16:24, 128:256])
    z1ps[3] = pb[5] - jnp.where(pick, part[8:16, 256:384], part[16:24, 256:384])
    z1.append(send(z1ps, z1pr, z_sem, 1, z_ids[0]))
    keep_p(3, p3)
    subtract(3, 4)
    wait(z1)

    p2[...] = z1ps[...] + z1pr[...]
    fc[c, me] = p2[0:2]
    ag_c = gather_all(p2.at[0:2], fc, agc_sem)
    scale = 4.0 / AGENTS
    inverse = invert(eye + (z1s[...] + z1r[...]) * scale) * scale
    wait(ag_c)
    m21 = block(fc, 0, slice(None), 0)
    m2 = jnp.concatenate([m21, block(fc, 0, slice(None), 1), block(fc, 1, slice(None), 0)], axis=1)
    pm2 = dot_full(inverse, m2)
    for k in range(2):
        pt[128 * k : 128 * k + 128, :] = pm2[:, 128 * k : 128 * k + 128].T
    z2s[...] = block(fc, 1, slice(None), 1) - dot_full(pt[0:128, :], m21)
    z2 = [send(z2s, z2r, z_sem, 2, z_ids[1])]
    left = jnp.concatenate([pt[pl.ds(pl.multiple_of(128 * k + 8 * me, 8), 8), :] for k in range(2)], axis=0)
    part = dot_full(left, m2[:, 128:])
    z2ps[0] = p2[2] - jnp.where(pick, part[0:8, 0:128], part[8:16, 0:128])
    z2ps[1] = p2[3] - jnp.where(pick, part[0:8, 128:256], part[8:16, 128:256])
    z2.append(send(z2ps, z2pr, z_sem, 3, z_ids[1]))
    keep_p(2, pm2)
    subtract(2, 3)
    wait(z2)

    p1[...] = z2ps[...] + z2pr[...]
    fd[c, me] = p1[...]
    ag_d = gather_all(p1, fd, agd_sem)
    scale = 2.0 / AGENTS
    inverse = invert(eye + (z2s[...] + z2r[...]) * scale) * scale
    wait(ag_d)
    m1 = jnp.concatenate([block(fd, 0, slice(None), 0), block(fd, 0, slice(None), 1)], axis=1)
    pm1 = dot_full(inverse, m1)
    m0 = jnp.concatenate([block(fd, 1, slice(None), 0), block(fd, 1, slice(None), 1)], axis=1)
    z4s[...] = m0 - dot_full(pm1[:, :128].T, m1)
    z4 = send(z4s, z4r, z_sem, 4, z_ids[2])
    keep_p(1, pm1)
    subtract(1, 2)
    z4.wait()

    m0 = z4s[...] + z4r[...]
    scale = 1.0 / AGENTS
    inverse = invert(eye + m0[:, :128] * scale) * scale
    keep_p(0, dot_full(inverse, m0[:, 128:]))
    subtract(0, 1)


def local(coupling, weights, rhs, order):
    def vmem(*shape, dtype=F32):
        return pltpu.VMEM(shape, dtype)

    def sems(n):
        return pltpu.SemaphoreType.DMA((2, n))

    whole = pl.BlockSpec(memory_space=pltpu.VMEM)
    anywhere = pl.BlockSpec(memory_space=pl.ANY)
    scalar = pl.BlockSpec(memory_space=pltpu.SMEM)
    applied, answer = pl.pallas_call(
        kernel,
        in_specs=[scalar, scalar, whole, anywhere, anywhere, anywhere, anywhere],
        out_specs=[whole, whole],
        out_shape=[
            jax.ShapeDtypeStruct((4 * ROWS, CAP), F32),
            jax.ShapeDtypeStruct((ROWS, CAP), F32),
        ],
        scratch_shapes=[
            vmem(4 * ROWS, CAP), vmem(ROWS, 4, CAP), vmem(ROWS, CAP), vmem(ROWS, 1, CAP), pltpu.SemaphoreType.DMA((10,)),
            vmem(ROWS, 640, dtype=BF), vmem(ROWS, 640, dtype=BF),
            vmem(ROWS, 512, dtype=BF), vmem(ROWS, 512, dtype=BF),
            vmem(16, 2, 8, 128), vmem(16, 2, 8, 128), vmem(16, 2, 8, 128),
            vmem(15, 2, 8, 128), vmem(2, 8, 128), vmem(16, 2, 8, 128),
            vmem(2, 16, 6, 8, 128), vmem(16, 6, 8, 128), vmem(16, 6, 8, 128),
            vmem(15, 6, 8, 128), vmem(6, 8, 128), vmem(2, 16, 2, 8, 128),
            vmem(128, 128), vmem(128, 128), vmem(4, 8, 128), vmem(4, 8, 128),
            vmem(4, 8, 128), vmem(2, 16, 2, 8, 128),
            vmem(128, 128), vmem(128, 128), vmem(2, 8, 128), vmem(2, 8, 128),
            vmem(2, 8, 128), vmem(2, 16, 2, 8, 128),
            vmem(128, 256), vmem(128, 256),
            vmem(128, 1280, dtype=BF), vmem(128, 1280, dtype=BF), vmem(384, 128),
            sems(2), sems(15), sems(15), sems(15), sems(31), sems(31), sems(31), sems(5),
        ],
        compiler_params=pltpu.CompilerParams(
            collective_id=0, has_side_effects=True, vmem_limit_bytes=56 * 2**20
        ),
        name="hodlr",
    )(
        order.reshape(ROWS),
        weights,
        weights.reshape(ROWS // 128, 128),
        coupling.reshape(4 * ROWS, CAP),
        coupling,
        rhs,
        rhs.reshape(ROWS, 1, CAP),
    )
    return applied.reshape(ROWS, 4, CAP), answer


def solution(mesh):
    rows = ("leaf", "sub")
    return jax.shard_map(
        local,
        mesh=mesh,
        in_specs=(P(rows, None, None), P(rows), P(rows, None), P(rows, None)),
        out_specs=(P(rows, None, None), P(rows, None)),
        check_vma=False,
    )
```

```python
import jax
import jax.numpy as jnp
from jax import lax
from jax.experimental import pallas as pl
from jax.experimental.pallas import tpu as pltpu
from jax.sharding import PartitionSpec as P

MESH = pl.DeviceIdType.MESH
F32 = jnp.float32
BF = jnp.bfloat16
ROWS = 2048
CAP = 128
AGENTS = 524288
CHUNK = 256


def split(x):
    head = x.astype(BF)
    return head, (x - head.astype(F32)).astype(BF)


def dot3(a, b, contract=((1,), (0,))):
    def one(p, q):
        return lax.dot_general(p, q, (contract, ((), ())), preferred_element_type=F32)

    return one(a[0], b[0]) + (one(a[0], b[1]) + one(a[1], b[0]))


def dot_full(a, b):
    return jnp.dot(a, b, precision=lax.Precision.HIGHEST, preferred_element_type=F32)


def sub_bcast(v, i):
    return jnp.broadcast_to(v[i : i + 1, :], (8, 128))


def lane_bcast(v, j):
    return jnp.broadcast_to(v[:, j : j + 1], (8, 128))


def lane_full(v, j):
    return jnp.maximum(lane_bcast(v, j), -3e38)


def recip(x):
    r = pltpu.reciprocal(x, approx=True)
    return r * (2.0 - x * r)


def eliminate_panel(cols, rows, ahead, off, lane, sub):
    cols, ahead = list(cols), list(ahead)
    out = jnp.where(
        (lane >= off) & (lane < off + 8), jnp.where(lane - off == sub, 1.0, 0.0), rows
    )
    for i in range(0, 8, 2):
        ci, cj = cols[i], cols[i + 1]
        a, b = sub_bcast(ci, i), sub_bcast(cj, i)
        b2, c = sub_bcast(ci, i + 1), sub_bcast(cj, i + 1)
        inv_det = recip(a * c - b * b2)
        n0 = jnp.where(sub == i, -c, jnp.where(sub == i + 1, b2, ci * c - cj * b2))
        n1 = jnp.where(sub == i, b, jnp.where(sub == i + 1, -a, cj * a - ci * b))
        f0, f1 = n0 * inv_det, n1 * inv_det
        keep = (sub != i) & (sub != i + 1)

        def update(v):
            return jnp.where(keep, v, 0.0) - (f0 * sub_bcast(v, i) + f1 * sub_bcast(v, i + 1))

        for j in range(i + 2, 8):
            cols[j] = update(cols[j])
        out = update(out)
        ahead = [update(v) for v in ahead]
    return out, ahead


def rank8(v, cols, rows):
    t = [cols[j] * rows[j] for j in range(8)]
    return v - (((t[0] + t[1]) + (t[2] + t[3])) + ((t[4] + t[5]) + (t[6] + t[7])))


def invert(matrix, block=8):
    s = [matrix[8 * q : 8 * q + 8, :] for q in range(16)]
    lane = lax.broadcasted_iota(jnp.int32, (8, 128), 1)
    sub = lax.broadcasted_iota(jnp.int32, (8, 128), 0)
    for first in range(0, 16, block):
        cols = [lane_full(s[first], 8 * first + j) for j in range(8)]
        for k in range(block):
            off = 8 * (first + k)
            inside = (lane >= off) & (lane < off + 8)
            last = k == block - 1
            rows = s[first + k]
            ahead = [] if last else [lane_full(rows, off + 8 + j) for j in range(8)]
            u, ahead = eliminate_panel(cols, rows, ahead, off, lane, sub)
            us = [sub_bcast(u, j) for j in range(8)]
            if not last:
                v = s[first + k + 1]
                lead = [lane_bcast(v, off + j) for j in range(8)]
                cols = [
                    rank8(lane_bcast(v, off + 8 + j), lead, [sub_bcast(ahead[j], i) for i in range(8)])
                    for j in range(8)
                ]
                s[first + k + 1] = rank8(jnp.where(inside, 0.0, v), lead, us)
            far = range(block - 1) if last else [(k + 2 + m) % block for m in range(block - 2)]
            for t in far:
                v = s[first + t]
                lead = [lane_bcast(v, off + j) for j in range(8)]
                s[first + t] = rank8(jnp.where(inside, 0.0, v), lead, us)
            s[first + k] = u
        rest = [(first + block + m) % 16 for m in range(16 - block)]
        left = jnp.concatenate([s[q] for q in rest], axis=0)
        left_lane = lax.broadcasted_iota(jnp.int32, left.shape, 1)
        inside = (left_lane >= 8 * first) & (left_lane < 8 * (first + block))
        parts = [jnp.zeros((8, 128), F32)] * 16
        parts[first : first + block] = s[first : first + block]
        wide = jnp.concatenate(parts, axis=0)
        new = jnp.where(inside, 0.0, left) - dot_full(jnp.where(inside, left, 0.0), wide)
        for m, q in enumerate(rest):
            s[q] = new[8 * m : 8 * m + 8]
    return jnp.concatenate(s, axis=0)


def kernel(
    order, w_s, w_v, coup_hbm, coup_rows_hbm, rhs_hbm, rhs_rows_hbm,
    applied_hbm, answer_hbm, p0h, p0l,
    coup, coup_rows, rhs, rhs_rows, in_sem, applied, answer, out_sem,
    xh, xl, wh, wl,
    ga, ra, rsa, pa, fa,
    gb, rb, rsb, pb, fb,
    gc, rc, rsc, pc, fc, fd,
    z1s, z1r, z1ps, z1pr, p2,
    z2s, z2r, z2ps, z2pr, p1,
    z4s, z4r, z4bs, z4br,
    ph, plo, pt,
    core_sem, rsa_sem, aga_sem, rsb_sem, agb_sem, rsc_sem, agc_sem, agd_sem, z_sem,
):
    leaf = lax.axis_index("leaf")
    x = lax.axis_index("sub")
    z, y, c = leaf // 8, (leaf // 2) % 4, leaf % 2
    me = x * 4 + y

    def device(px, py, pz, pc):
        return (pz * 8 + py * 2 + pc, px)

    plane = []
    for dx in range(4):
        for dy in range(4):
            if (dx, dy) != (0, 0):
                plane.append(((x + dx) % 4, (y + dy) % 4))
    core_id = device(x, y, z, 1 - c)
    plane_ids = [device(px, py, z, c) for px, py in plane]
    plane_q = [px * 4 + py for px, py in plane]

    def z_flip(bit):
        return device(x, y, z + bit - 2 * bit * ((z // bit) % 2), c)

    z_ids = [z_flip(1), z_flip(2), z_flip(4)]

    quarter = ROWS // 4
    loads = []
    for i in range(4):
        at, at4 = pl.ds(quarter * i, quarter), pl.ds(4 * quarter * i, 4 * quarter)
        loads.append(pltpu.make_async_copy(coup_hbm.at[at4], coup.at[at4], in_sem.at[i]))
        loads.append(pltpu.make_async_copy(rhs_hbm.at[at], rhs.at[at], in_sem.at[4 + i]))
    loads.append(pltpu.make_async_copy(coup_rows_hbm, coup_rows, in_sem.at[8]))
    loads.append(pltpu.make_async_copy(rhs_rows_hbm, rhs_rows, in_sem.at[9]))
    for copy in loads:
        copy.start()

    barrier = pltpu.get_barrier_semaphore()
    everyone = plane_ids + [core_id] + z_ids
    for d in everyone:
        pl.semaphore_signal(barrier, inc=1, device_id=d, device_id_type=MESH)

    def send(src, dst, sems, i, d):
        copy = pltpu.make_async_remote_copy(
            src_ref=src, dst_ref=dst, send_sem=sems.at[0, i], recv_sem=sems.at[1, i],
            device_id=d, device_id_type=MESH,
        )
        copy.start()
        return copy

    def wait(copies):
        for copy in copies:
            copy.wait()

    def scatter(src, dst, sems):
        return [send(src.at[q], dst.at[i], sems, i, d) for i, (q, d) in enumerate(zip(plane_q, plane_ids))]

    def gather(src, dst, sems):
        return [send(src, dst.at[me], sems, i, d) for i, d in enumerate(plane_ids)]

    weight_cols = jnp.concatenate([w_v[...], jnp.zeros((112, 128), F32)], axis=0).T
    for g in range(16):
        if g % 4 == 0:
            wait(loads[g // 2 : g // 2 + 2])
        r0 = 128 * g
        col = jnp.broadcast_to(weight_cols[:, g : g + 1], (128, 128))
        for k in range(4):
            j = 3 - k
            basis = coup[pl.ds(4 * r0 + k, 128, stride=4), :]
            h, l = split(basis)
            xh[r0 : r0 + 128, 128 * j : 128 * j + 128] = h
            xl[r0 : r0 + 128, 128 * j : 128 * j + 128] = l
            h, l = split(basis * col)
            wh[r0 : r0 + 128, 128 * j : 128 * j + 128] = h
            wl[r0 : r0 + 128, 128 * j : 128 * j + 128] = l
        h, l = split(rhs[r0 : r0 + 128, :])
        xh[r0 : r0 + 128, 512:640] = h
        xl[r0 : r0 + 128, 512:640] = l

    def gram(a0, a1, b0, b1):
        return dot3(
            (wh[:, a0:a1], wl[:, a0:a1]), (xh[:, b0:b1], xl[:, b0:b1]), ((0,), (0,))
        )

    def put(ref, first, value):
        for k in range(value.shape[1] // 128):
            ref[:, first + k] = value[:, 128 * k : 128 * k + 128].reshape(16, 8, 128)

    put(ga, 0, gram(0, 128, 0, 256))
    pl.semaphore_wait(barrier, len(everyone))
    core_a = send(ga, ra, core_sem, 0, core_id)
    put(gb, 0, gram(0, 128, 256, 640))
    put(gb, 3, gram(128, 256, 128, 256))
    core_b = send(gb, rb, core_sem, 1, core_id)
    core_a.wait()
    ga[...] = ga[...] + ra[...]
    rs_a = scatter(ga, rsa, rsa_sem)
    put(gc, 0, gram(128, 256, 256, 640))
    core_b.wait()
    gb[...] = gb[...] + rb[...]
    rs_b = scatter(gb, rsb, rsb_sem)
    m = gram(256, 512, 256, 640)
    put(gc, 3, m[:128])
    put(gc, 6, m[128:, 128:])
    core_c = send(gc, rc, core_sem, 2, core_id)
    wait(rs_a)
    pa[...] = ga[me] + jnp.sum(rsa[...], axis=0)
    fa[me] = pa[...]
    ag_a = gather(pa, fa, aga_sem)
    wait(rs_b)
    pb[...] = gb[me] + jnp.sum(rsb[...], axis=0)
    fb[me] = pb[...]
    ag_b = gather(pb, fb, agb_sem)
    core_c.wait()
    gc[...] = gc[...] + rc[...]
    rs_c = scatter(gc, rsc, rsc_sem)

    wait(loads[8:])

    def permute(t, carry):
        for u in range(8):
            i = t * 8 + u
            r = order[i]
            s = w_s[r]
            applied[pl.ds(pl.multiple_of(4 * i, 4), 4), :] = coup_rows[r] * s
            answer[pl.ds(i, 1), :] = rhs_rows[r] * s
        return carry

    lax.fori_loop(0, ROWS // 8, permute, 0)

    eye = jnp.where(
        lax.broadcasted_iota(jnp.int32, (128, 128), 0)
        == lax.broadcasted_iota(jnp.int32, (128, 128), 1),
        1.0,
        0.0,
    )

    def block(ref, k):
        return ref[:, k].reshape(128, 128)

    def blocks(ref, first, count):
        return jnp.concatenate([block(ref, first + k) for k in range(count)], axis=1)

    def inverse_of(lead, nodes):
        scale = nodes / AGENTS
        return invert(eye + lead * scale) * scale

    def offset(level):
        return sum(128 * (k + 1) for k in range(3, level, -1))

    def keep(level, p):
        h, l = split(p)
        ph[:, offset(level) : offset(level) + p.shape[1]] = h
        plo[:, offset(level) : offset(level) + p.shape[1]] = l

    def subtract(level):
        cut = slice(offset(level), offset(level) + 128 * (level + 1))

        def body(t, carry):
            r0 = pl.multiple_of(t * CHUNK, CHUNK)
            lead = split(applied[pl.ds(4 * r0 + level, CHUNK, stride=4), :])
            change = dot3(lead, (ph[:, cut], plo[:, cut]))
            for k in range(level):
                at = pl.ds(4 * r0 + level - 1 - k, CHUNK, stride=4)
                applied[at, :] = applied[at, :] - change[:, 128 * k : 128 * k + 128]
            at = pl.ds(r0, CHUNK)
            answer[at, :] = answer[at, :] - change[:, 128 * level :]
            return carry

        lax.fori_loop(0, ROWS // CHUNK, body, 0)

    def own_rows(count):
        rows = [pt[pl.ds(pl.multiple_of(128 * k + 8 * me, 8), 8), :] for k in range(count)]
        return jnp.concatenate(rows, axis=0)

    wait(ag_a)
    inverse = inverse_of(block(fa, 0), 8.0)
    wait(ag_b)
    m32 = block(fa, 1)
    m3 = jnp.concatenate([m32, blocks(fb, 0, 3)], axis=1)
    p3 = dot_full(inverse, m3)
    for k in range(3):
        pt[128 * k : 128 * k + 128, :] = p3[:, 128 * k : 128 * k + 128].T
    z1s[...] = block(fb, 3) - dot_full(pt[0:128, :], m32)
    z1 = send(z1s, z1r, z_sem, 0, z_ids[0])
    part = dot_full(own_rows(3), m3[:, 128:])
    wait(rs_c)
    pc[...] = gc[me] + jnp.sum(rsc[...], axis=0)
    where = [(0, 0), (0, 1), (0, 2), (1, 0), (1, 1), (1, 2), (2, 1), (2, 2)]
    for k, (i, j) in enumerate(where):
        z1ps[k] = pc[k] - part[8 * i : 8 * i + 8, 128 * j : 128 * j + 128]
    z1p = send(z1ps, z1pr, z_sem, 1, z_ids[0])
    keep(3, p3)
    subtract(3)
    z1p.wait()
    p2[...] = z1ps[...] + z1pr[...]
    fc[me] = p2[0:4]
    ag_c = gather(p2.at[0:4], fc, agc_sem)

    z1.wait()
    inverse = inverse_of(z1s[...] + z1r[...], 4.0)
    wait(ag_c)
    m2 = blocks(fc, 0, 3)
    pm2 = dot_full(inverse, m2)
    for k in range(2):
        pt[128 * k : 128 * k + 128, :] = pm2[:, 128 * k : 128 * k + 128].T
    z2s[...] = block(fc, 3) - dot_full(pt[0:128, :], m2[:, :128])
    z2 = send(z2s, z2r, z_sem, 2, z_ids[1])
    part = dot_full(own_rows(2), m2[:, 128:])
    for k, (i, j) in enumerate([(0, 0), (0, 1), (1, 0), (1, 1)]):
        z2ps[k] = p2[4 + k] - part[8 * i : 8 * i + 8, 128 * j : 128 * j + 128]
    z2p = send(z2ps, z2pr, z_sem, 3, z_ids[1])
    keep(2, pm2)
    subtract(2)
    z2p.wait()
    p1[...] = z2ps[...] + z2pr[...]
    fd[me] = p1[...]
    ag_d = gather(p1, fd, agd_sem)

    z2.wait()
    inverse = inverse_of(z2s[...] + z2r[...], 2.0)
    wait(ag_d)
    m1 = blocks(fd, 0, 2)
    pm1 = dot_full(inverse, m1)
    m0 = blocks(fd, 2, 2) - dot_full(pm1[:, :128].T, m1)
    z4s[...] = m0[:, :128]
    z4 = send(z4s, z4r, z_sem, 4, z_ids[2])
    z4bs[...] = m0[:, 128:]
    z4b = send(z4bs, z4br, z_sem, 5, z_ids[2])
    keep(1, pm1)
    subtract(1)
    outs = [
        pltpu.make_async_copy(applied, applied_hbm, out_sem.at[0]),
        pltpu.make_async_copy(answer, answer_hbm, out_sem.at[1]),
    ]
    for copy in outs:
        copy.start()

    z4.wait()
    inverse = inverse_of(z4s[...] + z4r[...], 1.0)
    z4b.wait()
    h, l = split(dot_full(inverse, z4bs[...] + z4br[...]))
    p0h[...] = h
    p0l[...] = l
    wait(outs)


PARTS = 8


def finish_kernel(applied_in, answer_in, p0h, p0l, applied_out, answer_out, buf, ans, in_sem, out_sem):
    rows = ROWS // PARTS
    ins, outs = [], []
    for i in range(PARTS):
        at, at4 = pl.ds(rows * i, rows), pl.ds(4 * rows * i, 4 * rows)
        ins.append((
            pltpu.make_async_copy(applied_in.at[at4], buf.at[at4], in_sem.at[0, i]),
            pltpu.make_async_copy(answer_in.at[at], ans.at[at], in_sem.at[1, i]),
        ))
        outs.append((
            pltpu.make_async_copy(buf.at[at4], applied_out.at[at4], out_sem.at[0, i]),
            pltpu.make_async_copy(ans.at[at], answer_out.at[at], out_sem.at[1, i]),
        ))
    for a, b in ins:
        a.start()
        b.start()
    for i in range(PARTS):
        ins[i][0].wait()
        outs[i][0].start()
        ins[i][1].wait()
        lead = split(buf[pl.ds(4 * rows * i, rows, stride=4), :])
        at = pl.ds(rows * i, rows)
        ans[at, :] = ans[at, :] - dot3(lead, (p0h[...], p0l[...]))
        outs[i][1].start()
    for a, b in outs:
        a.wait()
        b.wait()


def local(coupling, weights, rhs, order):
    def vmem(*shape, dtype=F32):
        return pltpu.VMEM(shape, dtype)

    def sems(n):
        return pltpu.SemaphoreType.DMA((2, n))

    whole = pl.BlockSpec(memory_space=pltpu.VMEM)
    scalar = pl.BlockSpec(memory_space=pltpu.SMEM)
    anywhere = pl.BlockSpec(memory_space=pl.ANY)
    results = [
        jax.ShapeDtypeStruct((4 * ROWS, CAP), F32),
        jax.ShapeDtypeStruct((ROWS, CAP), F32),
    ]
    last = [jax.ShapeDtypeStruct((CAP, CAP), BF)] * 2
    state = pl.pallas_call(
        kernel,
        in_specs=[scalar, scalar, whole, anywhere, anywhere, anywhere, anywhere],
        out_specs=[anywhere, anywhere, whole, whole],
        out_shape=results + last,
        scratch_shapes=[
            vmem(4 * ROWS, CAP), vmem(ROWS, 4, CAP), vmem(ROWS, CAP), vmem(ROWS, 1, CAP),
            pltpu.SemaphoreType.DMA((10,)),
            vmem(4 * ROWS, CAP), vmem(ROWS, CAP), pltpu.SemaphoreType.DMA((2,)),
            vmem(ROWS, 640, dtype=BF), vmem(ROWS, 640, dtype=BF),
            vmem(ROWS, 512, dtype=BF), vmem(ROWS, 512, dtype=BF),
            vmem(16, 2, 8, 128), vmem(16, 2, 8, 128), vmem(15, 2, 8, 128), vmem(2, 8, 128), vmem(16, 2, 8, 128),
            vmem(16, 4, 8, 128), vmem(16, 4, 8, 128), vmem(15, 4, 8, 128), vmem(4, 8, 128), vmem(16, 4, 8, 128),
            vmem(16, 8, 8, 128), vmem(16, 8, 8, 128), vmem(15, 8, 8, 128), vmem(8, 8, 128),
            vmem(16, 4, 8, 128), vmem(16, 4, 8, 128),
            vmem(128, 128), vmem(128, 128), vmem(8, 8, 128), vmem(8, 8, 128), vmem(8, 8, 128),
            vmem(128, 128), vmem(128, 128), vmem(4, 8, 128), vmem(4, 8, 128), vmem(4, 8, 128),
            vmem(128, 128), vmem(128, 128), vmem(128, 128), vmem(128, 128),
            vmem(128, 1280, dtype=BF), vmem(128, 1280, dtype=BF), vmem(384, 128),
            sems(3), sems(15), sems(15), sems(15), sems(15), sems(15), sems(15), sems(15), sems(6),
        ],
        compiler_params=pltpu.CompilerParams(
            collective_id=0, has_side_effects=True, vmem_limit_bytes=56 * 2**20
        ),
        name="hodlr",
    )(
        order.reshape(ROWS),
        weights,
        weights.reshape(ROWS // 128, 128),
        coupling.reshape(4 * ROWS, CAP),
        coupling,
        rhs,
        rhs.reshape(ROWS, 1, CAP),
    )
    applied, answer = pl.pallas_call(
        finish_kernel,
        in_specs=[anywhere, anywhere, whole, whole],
        out_specs=[anywhere, anywhere],
        out_shape=results,
        scratch_shapes=[
            vmem(4 * ROWS, CAP), vmem(ROWS, CAP),
            sems(PARTS), sems(PARTS),
        ],
        compiler_params=pltpu.CompilerParams(vmem_limit_bytes=56 * 2**20),
        name="finish",
    )(*state)
    return applied.reshape(ROWS, 4, CAP), answer


def solution(mesh):
    rows = ("leaf", "sub")
    return jax.shard_map(
        local,
        mesh=mesh,
        in_specs=(P(rows, None, None), P(rows), P(rows, None), P(rows, None)),
        out_specs=(P(rows, None, None), P(rows, None)),
        check_vma=False,
    )
```

```python
import jax
import jax.numpy as jnp
from jax import lax
from jax.experimental import pallas as pl
from jax.experimental.pallas import tpu as pltpu
from jax.sharding import PartitionSpec as P

MESH = pl.DeviceIdType.MESH
F32 = jnp.float32
BF = jnp.bfloat16
ROWS = 2048
CAP = 128
AGENTS = 524288
CHUNK = 256
EARLY = 1280


def split(x):
    head = x.astype(BF)
    return head, (x - head.astype(F32)).astype(BF)


def dot3(a, b, contract=((1,), (0,))):
    def one(p, q):
        return lax.dot_general(p, q, (contract, ((), ())), preferred_element_type=F32)

    return one(a[0], b[0]) + (one(a[0], b[1]) + one(a[1], b[0]))


def dot_full(a, b):
    return jnp.dot(a, b, precision=lax.Precision.HIGHEST, preferred_element_type=F32)


def sub_bcast(v, i):
    return jnp.broadcast_to(v[i : i + 1, :], (8, 128))


def lane_bcast(v, j):
    return jnp.broadcast_to(v[:, j : j + 1], (8, 128))


def lane_full(v, j):
    return jnp.maximum(lane_bcast(v, j), -3e38)


def recip(x):
    r = pltpu.reciprocal(x, approx=True)
    return r * (2.0 - x * r)


def eliminate_panel(cols, rows, ahead, off, lane, sub):
    cols, ahead = list(cols), list(ahead)
    out = jnp.where(
        (lane >= off) & (lane < off + 8), jnp.where(lane - off == sub, 1.0, 0.0), rows
    )
    for i in range(0, 8, 2):
        ci, cj = cols[i], cols[i + 1]
        a, b = sub_bcast(ci, i), sub_bcast(cj, i)
        b2, c = sub_bcast(ci, i + 1), sub_bcast(cj, i + 1)
        inv_det = recip(a * c - b * b2)
        n0 = jnp.where(sub == i, -c, jnp.where(sub == i + 1, b2, ci * c - cj * b2))
        n1 = jnp.where(sub == i, b, jnp.where(sub == i + 1, -a, cj * a - ci * b))
        f0, f1 = n0 * inv_det, n1 * inv_det
        keep = (sub != i) & (sub != i + 1)

        def update(v):
            return jnp.where(keep, v, 0.0) - (f0 * sub_bcast(v, i) + f1 * sub_bcast(v, i + 1))

        for j in range(i + 2, 8):
            cols[j] = update(cols[j])
        out = update(out)
        ahead = [update(v) for v in ahead]
    return out, ahead


def rank8(v, cols, rows):
    t = [cols[j] * rows[j] for j in range(8)]
    return v - (((t[0] + t[1]) + (t[2] + t[3])) + ((t[4] + t[5]) + (t[6] + t[7])))


def invert(matrix, block=8):
    s = [matrix[8 * q : 8 * q + 8, :] for q in range(16)]
    lane = lax.broadcasted_iota(jnp.int32, (8, 128), 1)
    sub = lax.broadcasted_iota(jnp.int32, (8, 128), 0)
    for first in range(0, 16, block):
        cols = [lane_full(s[first], 8 * first + j) for j in range(8)]
        for k in range(block):
            off = 8 * (first + k)
            inside = (lane >= off) & (lane < off + 8)
            last = k == block - 1
            rows = s[first + k]
            ahead = [] if last else [lane_full(rows, off + 8 + j) for j in range(8)]
            u, ahead = eliminate_panel(cols, rows, ahead, off, lane, sub)
            us = [sub_bcast(u, j) for j in range(8)]
            if not last:
                v = s[first + k + 1]
                lead = [lane_bcast(v, off + j) for j in range(8)]
                cols = [
                    rank8(lane_bcast(v, off + 8 + j), lead, [sub_bcast(ahead[j], i) for i in range(8)])
                    for j in range(8)
                ]
                s[first + k + 1] = rank8(jnp.where(inside, 0.0, v), lead, us)
            far = range(block - 1) if last else [(k + 2 + m) % block for m in range(block - 2)]
            for t in far:
                v = s[first + t]
                lead = [lane_bcast(v, off + j) for j in range(8)]
                s[first + t] = rank8(jnp.where(inside, 0.0, v), lead, us)
            s[first + k] = u
        rest = [(first + block + m) % 16 for m in range(16 - block)]
        left = jnp.concatenate([s[q] for q in rest], axis=0)
        left_lane = lax.broadcasted_iota(jnp.int32, left.shape, 1)
        inside = (left_lane >= 8 * first) & (left_lane < 8 * (first + block))
        parts = [jnp.zeros((8, 128), F32)] * 16
        parts[first : first + block] = s[first : first + block]
        wide = jnp.concatenate(parts, axis=0)
        new = jnp.where(inside, 0.0, left) - dot_full(jnp.where(inside, left, 0.0), wide)
        for m, q in enumerate(rest):
            s[q] = new[8 * m : 8 * m + 8]
    return jnp.concatenate(s, axis=0)


def kernel(
    order, w_s, w_v, coup_hbm, coup_rows_hbm, rhs_hbm, rhs_rows_hbm,
    applied_out, answer_out, a0h_out, a0l_out, p0h, p0l,
    coup, coup_rows, rhs, rhs_rows, in_sem, applied, answer, a0h, a0l, out_sem,
    xh, xl, wh, wl,
    ga, ra, rsa, pa, fa,
    gb, rb, rsb, pb, fb,
    gc, rc, rsc, pc, fc, fd,
    z1s, z1r, z1ps, z1pr, p2,
    z2s, z2r, z2ps, z2pr, p1,
    z4s, z4r, z4bs, z4br,
    ph, plo, mt,
    core_sem, rsa_sem, aga_sem, rsb_sem, agb_sem, rsc_sem, agc_sem, agd_sem, z_sem,
):
    leaf = lax.axis_index("leaf")
    x = lax.axis_index("sub")
    z, y, c = leaf // 8, (leaf // 2) % 4, leaf % 2
    me = x * 4 + y

    def device(px, py, pz, pc):
        return (pz * 8 + py * 2 + pc, px)

    plane = []
    for dx in range(4):
        for dy in range(4):
            if (dx, dy) != (0, 0):
                plane.append(((x + dx) % 4, (y + dy) % 4))
    core_id = device(x, y, z, 1 - c)
    plane_ids = [device(px, py, z, c) for px, py in plane]
    plane_q = [px * 4 + py for px, py in plane]

    def z_flip(bit):
        return device(x, y, z + bit - 2 * bit * ((z // bit) % 2), c)

    z_ids = [z_flip(1), z_flip(2), z_flip(4)]

    quarter = ROWS // 4
    loads = []
    for i in range(4):
        at, at4 = pl.ds(quarter * i, quarter), pl.ds(4 * quarter * i, 4 * quarter)
        loads.append(pltpu.make_async_copy(coup_hbm.at[at4], coup.at[at4], in_sem.at[i]))
        loads.append(pltpu.make_async_copy(rhs_hbm.at[at], rhs.at[at], in_sem.at[4 + i]))
    loads.append(pltpu.make_async_copy(coup_rows_hbm, coup_rows, in_sem.at[8]))
    loads.append(pltpu.make_async_copy(rhs_rows_hbm, rhs_rows, in_sem.at[9]))
    for copy in loads:
        copy.start()

    barrier = pltpu.get_barrier_semaphore()
    everyone = plane_ids + [core_id] + z_ids
    for d in everyone:
        pl.semaphore_signal(barrier, inc=1, device_id=d, device_id_type=MESH)

    def send(src, dst, sems, i, d):
        copy = pltpu.make_async_remote_copy(
            src_ref=src, dst_ref=dst, send_sem=sems.at[0, i], recv_sem=sems.at[1, i],
            device_id=d, device_id_type=MESH,
        )
        copy.start()
        return copy

    def wait(copies):
        for copy in copies:
            copy.wait()

    def scatter(src, dst, sems):
        return [send(src.at[q], dst.at[i], sems, i, d) for i, (q, d) in enumerate(zip(plane_q, plane_ids))]

    def gather(src, dst, sems):
        return [send(src, dst.at[me], sems, i, d) for i, d in enumerate(plane_ids)]

    weight_cols = jnp.concatenate([w_v[...], jnp.zeros((112, 128), F32)], axis=0).T
    for g in range(16):
        if g % 4 == 0:
            wait(loads[g // 2 : g // 2 + 2])
        r0 = 128 * g
        col = jnp.broadcast_to(weight_cols[:, g : g + 1], (128, 128))
        for k in range(4):
            j = 3 - k
            basis = coup[pl.ds(4 * r0 + k, 128, stride=4), :]
            h, l = split(basis)
            xh[r0 : r0 + 128, 128 * j : 128 * j + 128] = h
            xl[r0 : r0 + 128, 128 * j : 128 * j + 128] = l
            h, l = split(basis * col)
            wh[r0 : r0 + 128, 128 * j : 128 * j + 128] = h
            wl[r0 : r0 + 128, 128 * j : 128 * j + 128] = l
        h, l = split(rhs[r0 : r0 + 128, :])
        xh[r0 : r0 + 128, 512:640] = h
        xl[r0 : r0 + 128, 512:640] = l

    def gram(a0, a1, b0, b1):
        return dot3(
            (wh[:, a0:a1], wl[:, a0:a1]), (xh[:, b0:b1], xl[:, b0:b1]), ((0,), (0,))
        )

    def put(ref, first, value):
        for k in range(value.shape[1] // 128):
            ref[:, first + k] = value[:, 128 * k : 128 * k + 128].reshape(16, 8, 128)

    put(ga, 0, gram(0, 128, 0, 256))
    pl.semaphore_wait(barrier, len(everyone))
    core_a = send(ga, ra, core_sem, 0, core_id)
    put(gb, 0, gram(0, 128, 256, 640))
    put(gb, 3, gram(128, 256, 128, 256))
    core_b = send(gb, rb, core_sem, 1, core_id)
    core_a.wait()
    ga[...] = ga[...] + ra[...]
    rs_a = scatter(ga, rsa, rsa_sem)
    put(gc, 0, gram(128, 256, 256, 640))
    core_b.wait()
    gb[...] = gb[...] + rb[...]
    rs_b = scatter(gb, rsb, rsb_sem)
    m = gram(256, 512, 256, 640)
    put(gc, 3, m[:128])
    put(gc, 6, m[128:, 128:])
    core_c = send(gc, rc, core_sem, 2, core_id)
    wait(rs_a)
    pa[...] = ga[me] + jnp.sum(rsa[...], axis=0)
    fa[me] = pa[...]
    ag_a = gather(pa, fa, aga_sem)
    wait(rs_b)
    pb[...] = gb[me] + jnp.sum(rsb[...], axis=0)
    fb[me] = pb[...]
    ag_b = gather(pb, fb, agb_sem)
    core_c.wait()
    gc[...] = gc[...] + rc[...]
    rs_c = scatter(gc, rsc, rsc_sem)

    wait(loads[8:])

    def permute(t, carry):
        for u in range(8):
            i = t * 8 + u
            r = order[i]
            s = w_s[r]
            applied[pl.ds(pl.multiple_of(4 * i, 4), 4), :] = coup_rows[r] * s
            answer[pl.ds(i, 1), :] = rhs_rows[r] * s
        return carry

    lax.fori_loop(0, EARLY // 8, permute, 0)

    eye = jnp.where(
        lax.broadcasted_iota(jnp.int32, (128, 128), 0)
        == lax.broadcasted_iota(jnp.int32, (128, 128), 1),
        1.0,
        0.0,
    )

    def block(ref, k):
        return ref[:, k].reshape(128, 128)

    def blocks(ref, first, count):
        return jnp.concatenate([block(ref, first + k) for k in range(count)], axis=1)

    def inverse_of(lead, nodes):
        scale = nodes / AGENTS
        return invert(eye + lead * scale) * scale

    def offset(level):
        return sum(128 * (k + 1) for k in range(3, level, -1))

    def keep(level, p):
        h, l = split(p)
        ph[:, offset(level) : offset(level) + p.shape[1]] = h
        plo[:, offset(level) : offset(level) + p.shape[1]] = l

    def subtract(level):
        cut = slice(offset(level), offset(level) + 128 * (level + 1))

        def body(t, carry):
            r0 = pl.multiple_of(t * CHUNK, CHUNK)
            lead = split(applied[pl.ds(4 * r0 + level, CHUNK, stride=4), :])
            change = dot3(lead, (ph[:, cut], plo[:, cut]))
            for k in range(level):
                at = pl.ds(4 * r0 + level - 1 - k, CHUNK, stride=4)
                applied[at, :] = applied[at, :] - change[:, 128 * k : 128 * k + 128]
            at = pl.ds(r0, CHUNK)
            answer[at, :] = answer[at, :] - change[:, 128 * level :]
            return carry

        lax.fori_loop(0, ROWS // CHUNK, body, 0)

    def turn(ref, first, count):
        for k in range(count):
            mt[128 * k : 128 * k + 128, :] = block(ref, first + k).T

    def reduced(inverse, count, lead, rest):
        own = [mt[pl.ds(pl.multiple_of(128 * k + 8 * me, 8), 8), :] for k in range(count)]
        left = dot_full(jnp.concatenate([mt[0:128, :]] + own, axis=0), inverse)
        return dot_full(left[:128], lead), dot_full(left[128:], rest)

    wait(ag_a)
    turn(fa, 1, 1)
    inverse = inverse_of(block(fa, 0), 8.0)
    wait(ag_b)
    for k in range(2):
        mt[128 * k + 128 : 128 * k + 256, :] = block(fb, k).T
    m32 = block(fa, 1)
    rest = blocks(fb, 0, 3)
    full, part = reduced(inverse, 3, m32, rest)
    wait(rs_c)
    pc[...] = gc[me] + jnp.sum(rsc[...], axis=0)
    where = [(0, 0), (0, 1), (0, 2), (1, 0), (1, 1), (1, 2), (2, 1), (2, 2)]
    for k, (i, j) in enumerate(where):
        z1ps[k] = pc[k] - part[8 * i : 8 * i + 8, 128 * j : 128 * j + 128]
    z1p = send(z1ps, z1pr, z_sem, 1, z_ids[0])
    z1s[...] = block(fb, 3) - full
    z1 = send(z1s, z1r, z_sem, 0, z_ids[0])
    keep(3, dot_full(inverse, jnp.concatenate([m32, rest], axis=1)))
    lax.fori_loop(EARLY // 8, ROWS // 8, permute, 0)
    z1p.wait()
    p2[...] = z1ps[...] + z1pr[...]
    fc[me] = p2[0:4]
    ag_c = gather(p2.at[0:4], fc, agc_sem)

    z1.wait()
    inverse = inverse_of(z1s[...] + z1r[...], 4.0)
    subtract(3)
    wait(ag_c)
    turn(fc, 0, 2)
    m21 = block(fc, 0)
    rest = blocks(fc, 1, 2)
    full, part = reduced(inverse, 2, m21, rest)
    for k, (i, j) in enumerate([(0, 0), (0, 1), (1, 0), (1, 1)]):
        z2ps[k] = p2[4 + k] - part[8 * i : 8 * i + 8, 128 * j : 128 * j + 128]
    z2p = send(z2ps, z2pr, z_sem, 3, z_ids[1])
    z2s[...] = block(fc, 3) - full
    z2 = send(z2s, z2r, z_sem, 2, z_ids[1])
    keep(2, dot_full(inverse, jnp.concatenate([m21, rest], axis=1)))
    subtract(2)
    z2p.wait()
    p1[...] = z2ps[...] + z2pr[...]
    fd[me] = p1[...]
    ag_d = gather(p1, fd, agd_sem)

    z2.wait()
    inverse = inverse_of(z2s[...] + z2r[...], 2.0)
    wait(ag_d)
    turn(fd, 0, 1)
    m1 = blocks(fd, 0, 2)
    m0 = blocks(fd, 2, 2) - dot_full(dot_full(mt[0:128, :], inverse), m1)
    z4s[...] = m0[:, :128]
    z4 = send(z4s, z4r, z_sem, 4, z_ids[2])
    z4bs[...] = m0[:, 128:]
    z4b = send(z4bs, z4br, z_sem, 5, z_ids[2])
    keep(1, dot_full(inverse, m1))
    subtract(1)
    h, l = split(applied[pl.ds(0, ROWS, stride=4), :])
    a0h[...] = h
    a0l[...] = l
    outs = [
        pltpu.make_async_copy(a, b, out_sem.at[i])
        for i, (a, b) in enumerate(
            [(applied, applied_out), (answer, answer_out), (a0h, a0h_out), (a0l, a0l_out)]
        )
    ]
    for copy in outs:
        copy.start()

    z4.wait()
    inverse = inverse_of(z4s[...] + z4r[...], 1.0)
    z4b.wait()
    h, l = split(dot_full(inverse, z4bs[...] + z4br[...]))
    p0h[...] = h
    p0l[...] = l
    wait(outs)


PARTS = 8


def finish_kernel(applied_in, answer_in, a0h, a0l, p0h, p0l, applied_out, answer_out, ans, sem):
    rows = ROWS // PARTS
    outs = []
    for i in range(PARTS):
        at4 = pl.ds(4 * rows * i, 4 * rows)
        outs.append(pltpu.make_async_copy(applied_in.at[at4], applied_out.at[at4], sem.at[0, i]))
        outs[-1].start()
    for i in range(PARTS):
        at = pl.ds(rows * i, rows)
        ans[at, :] = answer_in[at, :] - dot3((a0h[at, :], a0l[at, :]), (p0h[...], p0l[...]))
        outs.append(pltpu.make_async_copy(ans.at[at], answer_out.at[at], sem.at[1, i]))
        outs[-1].start()
    for copy in outs:
        copy.wait()


def local(coupling, weights, rhs, order):
    def vmem(*shape, dtype=F32):
        return pltpu.VMEM(shape, dtype)

    def sems(n):
        return pltpu.SemaphoreType.DMA((2, n))

    whole = pl.BlockSpec(memory_space=pltpu.VMEM)
    scalar = pl.BlockSpec(memory_space=pltpu.SMEM)
    anywhere = pl.BlockSpec(memory_space=pl.ANY)
    results = [
        jax.ShapeDtypeStruct((4 * ROWS, CAP), F32),
        jax.ShapeDtypeStruct((ROWS, CAP), F32),
    ]
    last = [jax.ShapeDtypeStruct((ROWS, CAP), BF)] * 2 + [jax.ShapeDtypeStruct((CAP, CAP), BF)] * 2

    def in_hbm(v):
        return pltpu.with_memory_space_constraint(v, pltpu.HBM)

    state = pl.pallas_call(
        kernel,
        in_specs=[scalar, scalar, whole, anywhere, anywhere, anywhere, anywhere],
        out_specs=[anywhere] * 4 + [whole] * 2,
        out_shape=results + last,
        scratch_shapes=[
            vmem(4 * ROWS, CAP), vmem(ROWS, 4, CAP), vmem(ROWS, CAP), vmem(ROWS, 1, CAP),
            pltpu.SemaphoreType.DMA((10,)),
            vmem(4 * ROWS, CAP), vmem(ROWS, CAP), vmem(ROWS, CAP, dtype=BF), vmem(ROWS, CAP, dtype=BF),
            pltpu.SemaphoreType.DMA((4,)),
            vmem(ROWS, 640, dtype=BF), vmem(ROWS, 640, dtype=BF),
            vmem(ROWS, 512, dtype=BF), vmem(ROWS, 512, dtype=BF),
            vmem(16, 2, 8, 128), vmem(16, 2, 8, 128), vmem(15, 2, 8, 128), vmem(2, 8, 128), vmem(16, 2, 8, 128),
            vmem(16, 4, 8, 128), vmem(16, 4, 8, 128), vmem(15, 4, 8, 128), vmem(4, 8, 128), vmem(16, 4, 8, 128),
            vmem(16, 8, 8, 128), vmem(16, 8, 8, 128), vmem(15, 8, 8, 128), vmem(8, 8, 128),
            vmem(16, 4, 8, 128), vmem(16, 4, 8, 128),
            vmem(128, 128), vmem(128, 128), vmem(8, 8, 128), vmem(8, 8, 128), vmem(8, 8, 128),
            vmem(128, 128), vmem(128, 128), vmem(4, 8, 128), vmem(4, 8, 128), vmem(4, 8, 128),
            vmem(128, 128), vmem(128, 128), vmem(128, 128), vmem(128, 128),
            vmem(128, 1280, dtype=BF), vmem(128, 1280, dtype=BF), vmem(384, 128),
            sems(3), sems(15), sems(15), sems(15), sems(15), sems(15), sems(15), sems(15), sems(6),
        ],
        compiler_params=pltpu.CompilerParams(
            collective_id=0, has_side_effects=True, vmem_limit_bytes=44 * 2**20
        ),
        name="hodlr",
    )(
        in_hbm(order.reshape(ROWS)),
        in_hbm(weights),
        in_hbm(weights.reshape(ROWS // 128, 128)),
        in_hbm(coupling.reshape(4 * ROWS, CAP)),
        in_hbm(coupling),
        in_hbm(rhs),
        in_hbm(rhs.reshape(ROWS, 1, CAP)),
    )
    applied, answer = pl.pallas_call(
        finish_kernel,
        in_specs=[anywhere] + [whole] * 5,
        out_specs=[anywhere, anywhere],
        out_shape=results,
        scratch_shapes=[vmem(ROWS, CAP), sems(PARTS)],
        compiler_params=pltpu.CompilerParams(vmem_limit_bytes=16 * 2**20),
        name="finish",
    )(*state)
    return applied.reshape(ROWS, 4, CAP), answer


def solution(mesh):
    rows = ("leaf", "sub")
    return jax.shard_map(
        local,
        mesh=mesh,
        in_specs=(P(rows, None, None), P(rows), P(rows, None), P(rows, None)),
        out_specs=(P(rows, None, None), P(rows, None)),
        check_vma=False,
    )
```

```python
import jax
import jax.numpy as jnp
from jax import lax
from jax.experimental import pallas as pl
from jax.experimental.pallas import tpu as pltpu
from jax.sharding import PartitionSpec as P

MESH = pl.DeviceIdType.MESH
F32 = jnp.float32
BF = jnp.bfloat16
ROWS = 2048
CAP = 128
AGENTS = 524288
CHUNK = 256
EARLY = 1024


def split(x):
    head = x.astype(BF)
    return head, (x - head.astype(F32)).astype(BF)


def dot3(a, b, contract=((1,), (0,))):
    def one(p, q):
        return lax.dot_general(p, q, (contract, ((), ())), preferred_element_type=F32)

    return one(a[0], b[0]) + (one(a[0], b[1]) + one(a[1], b[0]))


def dot_full(a, b):
    return jnp.dot(a, b, precision=lax.Precision.HIGHEST, preferred_element_type=F32)


def sub_bcast(v, i):
    return jnp.broadcast_to(v[i : i + 1, :], (8, 128))


def lane_bcast(v, j):
    return jnp.broadcast_to(v[:, j : j + 1], (8, 128))


def lane_full(v, j):
    return jnp.maximum(lane_bcast(v, j), -3e38)


def recip(x):
    r = pltpu.reciprocal(x, approx=True)
    return r * (2.0 - x * r)


def eliminate_panel(cols, rows, ahead, off, lane, sub):
    cols, ahead = list(cols), list(ahead)
    out = jnp.where(
        (lane >= off) & (lane < off + 8), jnp.where(lane - off == sub, 1.0, 0.0), rows
    )
    for i in range(0, 8, 2):
        ci, cj = cols[i], cols[i + 1]
        a, b = sub_bcast(ci, i), sub_bcast(cj, i)
        b2, c = sub_bcast(ci, i + 1), sub_bcast(cj, i + 1)
        inv_det = recip(a * c - b * b2)
        n0 = jnp.where(sub == i, -c, jnp.where(sub == i + 1, b2, ci * c - cj * b2))
        n1 = jnp.where(sub == i, b, jnp.where(sub == i + 1, -a, cj * a - ci * b))
        f0, f1 = n0 * inv_det, n1 * inv_det
        keep = (sub != i) & (sub != i + 1)

        def update(v):
            return jnp.where(keep, v, 0.0) - (f0 * sub_bcast(v, i) + f1 * sub_bcast(v, i + 1))

        for j in range(i + 2, 8):
            cols[j] = update(cols[j])
        out = update(out)
        ahead = [update(v) for v in ahead]
    return out, ahead


def rank8(v, cols, rows):
    t = [cols[j] * rows[j] for j in range(8)]
    return v - (((t[0] + t[1]) + (t[2] + t[3])) + ((t[4] + t[5]) + (t[6] + t[7])))


def invert(matrix, block=8):
    s = [matrix[8 * q : 8 * q + 8, :] for q in range(16)]
    lane = lax.broadcasted_iota(jnp.int32, (8, 128), 1)
    sub = lax.broadcasted_iota(jnp.int32, (8, 128), 0)
    for first in range(0, 16, block):
        cols = [lane_full(s[first], 8 * first + j) for j in range(8)]
        for k in range(block):
            off = 8 * (first + k)
            inside = (lane >= off) & (lane < off + 8)
            last = k == block - 1
            rows = s[first + k]
            ahead = [] if last else [lane_full(rows, off + 8 + j) for j in range(8)]
            u, ahead = eliminate_panel(cols, rows, ahead, off, lane, sub)
            us = [sub_bcast(u, j) for j in range(8)]
            if not last:
                v = s[first + k + 1]
                lead = [lane_bcast(v, off + j) for j in range(8)]
                cols = [
                    rank8(lane_bcast(v, off + 8 + j), lead, [sub_bcast(ahead[j], i) for i in range(8)])
                    for j in range(8)
                ]
                s[first + k + 1] = rank8(jnp.where(inside, 0.0, v), lead, us)
            far = range(block - 1) if last else [(k + 2 + m) % block for m in range(block - 2)]
            for t in far:
                v = s[first + t]
                lead = [lane_bcast(v, off + j) for j in range(8)]
                s[first + t] = rank8(jnp.where(inside, 0.0, v), lead, us)
            s[first + k] = u
        rest = [(first + block + m) % 16 for m in range(16 - block)]
        left = jnp.concatenate([s[q] for q in rest], axis=0)
        left_lane = lax.broadcasted_iota(jnp.int32, left.shape, 1)
        inside = (left_lane >= 8 * first) & (left_lane < 8 * (first + block))
        parts = [jnp.zeros((8, 128), F32)] * 16
        parts[first : first + block] = s[first : first + block]
        wide = jnp.concatenate(parts, axis=0)
        new = jnp.where(inside, 0.0, left) - dot_full(jnp.where(inside, left, 0.0), wide)
        for m, q in enumerate(rest):
            s[q] = new[8 * m : 8 * m + 8]
    return jnp.concatenate(s, axis=0)


def kernel(
    order, w_s, w_v, coup_hbm, coup_rows_hbm, rhs_hbm, rhs_rows_hbm,
    applied_out, answer_out, a0h_out, a0l_out, p0h, p0l,
    coup, coup_rows, rhs, rhs_rows, in_sem, applied, answer, a0h, a0l, out_sem,
    xh, xl, wh, wl,
    ga, ra, rsa, pa, fa,
    gb, rb, rsb, pb, fb,
    gc, rc, rsc, pc, fc, fd,
    z1s, z1r, z1ps, z1pr, p2,
    z2s, z2r, z2ps, z2pr, p1,
    z4s, z4r, z4bs, z4br,
    ph, plo, mt,
    core_sem, rsa_sem, aga_sem, rsb_sem, agb_sem, rsc_sem, agc_sem, agd_sem, z_sem,
):
    leaf = lax.axis_index("leaf")
    x = lax.axis_index("sub")
    z, y, c = leaf // 8, (leaf // 2) % 4, leaf % 2
    me = x * 4 + y

    def device(px, py, pz, pc):
        return (pz * 8 + py * 2 + pc, px)

    plane = []
    for dx in range(4):
        for dy in range(4):
            if (dx, dy) != (0, 0):
                plane.append((abs(2 - dx) + abs(2 - dy), dx, dy))
    plane = [((x + dx) % 4, (y + dy) % 4) for _, dx, dy in sorted(plane)]
    core_id = device(x, y, z, 1 - c)
    plane_ids = [device(px, py, z, c) for px, py in plane]
    plane_q = [px * 4 + py for px, py in plane]

    def z_flip(bit):
        return device(x, y, z + bit - 2 * bit * ((z // bit) % 2), c)

    z_ids = [z_flip(1), z_flip(2), z_flip(4)]

    quarter = ROWS // 4
    loads = []
    for i in range(4):
        at, at4 = pl.ds(quarter * i, quarter), pl.ds(4 * quarter * i, 4 * quarter)
        loads.append(pltpu.make_async_copy(coup_hbm.at[at4], coup.at[at4], in_sem.at[i]))
        loads.append(pltpu.make_async_copy(rhs_hbm.at[at], rhs.at[at], in_sem.at[4 + i]))
    loads.append(pltpu.make_async_copy(coup_rows_hbm, coup_rows, in_sem.at[8]))
    loads.append(pltpu.make_async_copy(rhs_rows_hbm, rhs_rows, in_sem.at[9]))
    for copy in loads[:8]:
        copy.start()

    barrier = pltpu.get_barrier_semaphore()
    everyone = plane_ids + [core_id] + z_ids
    for d in everyone:
        pl.semaphore_signal(barrier, inc=1, device_id=d, device_id_type=MESH)

    def send(src, dst, sems, i, d):
        copy = pltpu.make_async_remote_copy(
            src_ref=src, dst_ref=dst, send_sem=sems.at[0, i], recv_sem=sems.at[1, i],
            device_id=d, device_id_type=MESH,
        )
        copy.start()
        return copy

    def wait(copies):
        for copy in copies:
            copy.wait()

    def scatter(src, dst, sems):
        return [send(src.at[q], dst.at[i], sems, i, d) for i, (q, d) in enumerate(zip(plane_q, plane_ids))]

    def gather(src, dst, sems):
        return [send(src, dst.at[me], sems, i, d) for i, d in enumerate(plane_ids)]

    weight_cols = jnp.concatenate([w_v[...], jnp.zeros((112, 128), F32)], axis=0).T
    for g in range(16):
        if g % 4 == 0:
            wait(loads[g // 2 : g // 2 + 2])
        r0 = 128 * g
        col = jnp.broadcast_to(weight_cols[:, g : g + 1], (128, 128))
        for k in range(4):
            j = 3 - k
            basis = coup[pl.ds(4 * r0 + k, 128, stride=4), :]
            h, l = split(basis)
            xh[r0 : r0 + 128, 128 * j : 128 * j + 128] = h
            xl[r0 : r0 + 128, 128 * j : 128 * j + 128] = l
            h, l = split(basis * col)
            wh[r0 : r0 + 128, 128 * j : 128 * j + 128] = h
            wl[r0 : r0 + 128, 128 * j : 128 * j + 128] = l
        h, l = split(rhs[r0 : r0 + 128, :])
        xh[r0 : r0 + 128, 512:640] = h
        xl[r0 : r0 + 128, 512:640] = l

    for copy in loads[8:]:
        copy.start()

    def gram(a0, a1, b0, b1):
        return dot3(
            (wh[:, a0:a1], wl[:, a0:a1]), (xh[:, b0:b1], xl[:, b0:b1]), ((0,), (0,))
        )

    def pieces(value):
        return value.reshape(16, 8, 128)

    def put(ref, first, value):
        for k in range(value.shape[1] // 128):
            ref[:, first + k] = pieces(value[:, 128 * k : 128 * k + 128])

    put(ga, 0, gram(0, 128, 0, 256))
    pl.semaphore_wait(barrier, len(everyone))
    core_a = send(ga, ra, core_sem, 0, core_id)
    put(gb, 0, gram(0, 128, 256, 640))
    core_a.wait()
    ga[...] = ga[...] + ra[...]
    rs_a = scatter(ga, rsa, rsa_sem)
    put(gb, 3, gram(128, 256, 128, 256))
    core_b = send(gb, rb, core_sem, 1, core_id)
    m = gram(128, 256, 256, 640)
    for k in range(3):
        gc[0, :, k] = pieces(m[:, 128 * k : 128 * k + 128])
    core_b.wait()
    gb[...] = gb[...] + rb[...]
    rs_b = scatter(gb, rsb, rsb_sem)
    m = gram(256, 512, 256, 640)
    gc[0, :, 3] = pieces(m[:128, :128])
    gc[1, :, 0] = pieces(m[:128, 128:256])
    gc[1, :, 1] = pieces(m[:128, 256:])
    gc[1, :, 2] = pieces(m[128:, 128:256])
    gc[1, :, 3] = pieces(m[128:, 256:])
    core_c = send(gc.at[1 - c], rc, core_sem, 2, core_id)
    wait(rs_a)
    pa[...] = ga[me] + jnp.sum(rsa[...], axis=0)
    fa[me] = pa[...]
    ag_a = gather(pa, fa, aga_sem)
    core_c.wait()
    rc[...] = rc[...] + gc[c]
    rs_c = scatter(rc, rsc, rsc_sem)
    wait(rs_b)
    pb[...] = gb[me] + jnp.sum(rsb[...], axis=0)
    fb[me] = pb[...]
    ag_b = gather(pb, fb, agb_sem)

    wait(loads[8:])

    def permute(t, carry):
        for u in range(8):
            i = t * 8 + u
            r = order[i]
            s = w_s[r]
            applied[pl.ds(pl.multiple_of(4 * i, 4), 4), :] = coup_rows[r] * s
            answer[pl.ds(i, 1), :] = rhs_rows[r] * s
        return carry

    lax.fori_loop(0, EARLY // 8, permute, 0)

    eye = jnp.where(
        lax.broadcasted_iota(jnp.int32, (128, 128), 0)
        == lax.broadcasted_iota(jnp.int32, (128, 128), 1),
        1.0,
        0.0,
    )

    def block(ref, k):
        return ref[:, k].reshape(128, 128)

    def blocks(ref, first, count):
        return jnp.concatenate([block(ref, first + k) for k in range(count)], axis=1)

    def inverse_of(lead, nodes):
        scale = nodes / AGENTS
        return invert(eye + lead * scale) * scale

    def offset(level):
        return sum(128 * (k + 1) for k in range(3, level, -1))

    def keep(level, p):
        h, l = split(p)
        ph[:, offset(level) : offset(level) + p.shape[1]] = h
        plo[:, offset(level) : offset(level) + p.shape[1]] = l

    def subtract(level):
        cut = slice(offset(level), offset(level) + 128 * (level + 1))

        def body(t, carry):
            r0 = pl.multiple_of(t * CHUNK, CHUNK)
            lead = split(applied[pl.ds(4 * r0 + level, CHUNK, stride=4), :])
            change = dot3(lead, (ph[:, cut], plo[:, cut]))
            for k in range(level):
                at = pl.ds(4 * r0 + level - 1 - k, CHUNK, stride=4)
                applied[at, :] = applied[at, :] - change[:, 128 * k : 128 * k + 128]
            at = pl.ds(r0, CHUNK)
            answer[at, :] = answer[at, :] - change[:, 128 * level :]
            return carry

        lax.fori_loop(0, ROWS // CHUNK, body, 0)

    def turn(ref, first, count):
        for k in range(count):
            mt[128 * k : 128 * k + 128, :] = block(ref, first + k).T

    def reduced(inverse, count, lead, rest):
        own = [mt[pl.ds(pl.multiple_of(128 * k + 8 * me, 8), 8), :] for k in range(count)]
        left = dot_full(jnp.concatenate([mt[0:128, :]] + own, axis=0), inverse)
        return dot_full(left[:128], lead), dot_full(left[128:], rest)

    wait(ag_a)
    turn(fa, 1, 1)
    inverse = inverse_of(block(fa, 0), 8.0)
    wait(rs_c)
    pc[c] = rc[me] + jnp.sum(rsc[...], axis=0)
    core_p = send(pc.at[c], pc.at[c], core_sem, 3, core_id)
    wait(ag_b)
    for k in range(2):
        mt[128 * k + 128 : 128 * k + 256, :] = block(fb, k).T
    m32 = block(fa, 1)
    rest = blocks(fb, 0, 3)
    full, part = reduced(inverse, 3, m32, rest)
    core_p.wait()
    where = [(0, 0), (0, 1), (0, 2), (1, 0), (1, 1), (1, 2), (2, 1), (2, 2)]
    for k, (i, j) in enumerate(where):
        z1ps[k] = pc[k // 4, k % 4] - part[8 * i : 8 * i + 8, 128 * j : 128 * j + 128]
    z1p = send(z1ps, z1pr, z_sem, 1, z_ids[0])
    z1s[...] = block(fb, 3) - full
    z1 = send(z1s, z1r, z_sem, 0, z_ids[0])
    keep(3, dot_full(inverse, jnp.concatenate([m32, rest], axis=1)))
    lax.fori_loop(EARLY // 8, ROWS // 8, permute, 0)
    z1p.wait()
    p2[...] = z1ps[...] + z1pr[...]
    fc[me] = p2[0:4]
    ag_c = gather(p2.at[0:4], fc, agc_sem)

    z1.wait()
    inverse = inverse_of(z1s[...] + z1r[...], 4.0)
    subtract(3)
    wait(ag_c)
    turn(fc, 0, 2)
    m21 = block(fc, 0)
    rest = blocks(fc, 1, 2)
    full, part = reduced(inverse, 2, m21, rest)
    for k, (i, j) in enumerate([(0, 0), (0, 1), (1, 0), (1, 1)]):
        z2ps[k] = p2[4 + k] - part[8 * i : 8 * i + 8, 128 * j : 128 * j + 128]
    z2p = send(z2ps, z2pr, z_sem, 3, z_ids[1])
    z2s[...] = block(fc, 3) - full
    z2 = send(z2s, z2r, z_sem, 2, z_ids[1])
    keep(2, dot_full(inverse, jnp.concatenate([m21, rest], axis=1)))
    subtract(2)
    z2p.wait()
    p1[...] = z2ps[...] + z2pr[...]
    fd[me] = p1[...]
    ag_d = gather(p1, fd, agd_sem)

    z2.wait()
    inverse = inverse_of(z2s[...] + z2r[...], 2.0)
    wait(ag_d)
    turn(fd, 0, 1)
    m1 = blocks(fd, 0, 2)
    m0 = blocks(fd, 2, 2) - dot_full(dot_full(mt[0:128, :], inverse), m1)
    z4s[...] = m0[:, :128]
    z4 = send(z4s, z4r, z_sem, 4, z_ids[2])
    z4bs[...] = m0[:, 128:]
    z4b = send(z4bs, z4br, z_sem, 5, z_ids[2])
    keep(1, dot_full(inverse, m1))
    subtract(1)
    h, l = split(applied[pl.ds(0, ROWS, stride=4), :])
    a0h[...] = h
    a0l[...] = l
    outs = [
        pltpu.make_async_copy(a, b, out_sem.at[i])
        for i, (a, b) in enumerate(
            [(applied, applied_out), (answer, answer_out), (a0h, a0h_out), (a0l, a0l_out)]
        )
    ]
    for copy in outs:
        copy.start()

    z4.wait()
    inverse = inverse_of(z4s[...] + z4r[...], 1.0)
    z4b.wait()
    h, l = split(dot_full(inverse, z4bs[...] + z4br[...]))
    p0h[...] = h
    p0l[...] = l
    wait(outs)


PARTS = 8


def finish_kernel(applied_in, answer_in, a0h, a0l, p0h, p0l, applied_out, answer_out, ans, sem):
    rows = ROWS // PARTS
    outs = []
    for i in range(PARTS):
        at4 = pl.ds(4 * rows * i, 4 * rows)
        outs.append(pltpu.make_async_copy(applied_in.at[at4], applied_out.at[at4], sem.at[0, i]))
        outs[-1].start()
    for i in range(PARTS):
        at = pl.ds(rows * i, rows)
        ans[at, :] = answer_in[at, :] - dot3((a0h[at, :], a0l[at, :]), (p0h[...], p0l[...]))
        outs.append(pltpu.make_async_copy(ans.at[at], answer_out.at[at], sem.at[1, i]))
        outs[-1].start()
    for copy in outs:
        copy.wait()


def local(coupling, weights, rhs, order):
    def vmem(*shape, dtype=F32):
        return pltpu.VMEM(shape, dtype)

    def sems(n):
        return pltpu.SemaphoreType.DMA((2, n))

    whole = pl.BlockSpec(memory_space=pltpu.VMEM)
    scalar = pl.BlockSpec(memory_space=pltpu.SMEM)
    anywhere = pl.BlockSpec(memory_space=pl.ANY)
    results = [
        jax.ShapeDtypeStruct((4 * ROWS, CAP), F32),
        jax.ShapeDtypeStruct((ROWS, CAP), F32),
    ]
    last = [jax.ShapeDtypeStruct((ROWS, CAP), BF)] * 2 + [jax.ShapeDtypeStruct((CAP, CAP), BF)] * 2

    def in_hbm(v):
        return pltpu.with_memory_space_constraint(v, pltpu.HBM)

    state = pl.pallas_call(
        kernel,
        in_specs=[scalar, scalar, whole, anywhere, anywhere, anywhere, anywhere],
        out_specs=[anywhere] * 4 + [whole] * 2,
        out_shape=results + last,
        scratch_shapes=[
            vmem(4 * ROWS, CAP), vmem(ROWS, 4, CAP), vmem(ROWS, CAP), vmem(ROWS, 1, CAP),
            pltpu.SemaphoreType.DMA((10,)),
            vmem(4 * ROWS, CAP), vmem(ROWS, CAP), vmem(ROWS, CAP, dtype=BF), vmem(ROWS, CAP, dtype=BF),
            pltpu.SemaphoreType.DMA((4,)),
            vmem(ROWS, 640, dtype=BF), vmem(ROWS, 640, dtype=BF),
            vmem(ROWS, 512, dtype=BF), vmem(ROWS, 512, dtype=BF),
            vmem(16, 2, 8, 128), vmem(16, 2, 8, 128), vmem(15, 2, 8, 128), vmem(2, 8, 128), vmem(16, 2, 8, 128),
            vmem(16, 4, 8, 128), vmem(16, 4, 8, 128), vmem(15, 4, 8, 128), vmem(4, 8, 128), vmem(16, 4, 8, 128),
            vmem(2, 16, 4, 8, 128), vmem(16, 4, 8, 128), vmem(15, 4, 8, 128), vmem(2, 4, 8, 128),
            vmem(16, 4, 8, 128), vmem(16, 4, 8, 128),
            vmem(128, 128), vmem(128, 128), vmem(8, 8, 128), vmem(8, 8, 128), vmem(8, 8, 128),
            vmem(128, 128), vmem(128, 128), vmem(4, 8, 128), vmem(4, 8, 128), vmem(4, 8, 128),
            vmem(128, 128), vmem(128, 128), vmem(128, 128), vmem(128, 128),
            vmem(128, 1280, dtype=BF), vmem(128, 1280, dtype=BF), vmem(384, 128),
            sems(4), sems(15), sems(15), sems(15), sems(15), sems(15), sems(15), sems(15), sems(6),
        ],
        compiler_params=pltpu.CompilerParams(
            collective_id=0, has_side_effects=True, vmem_limit_bytes=44 * 2**20
        ),
        name="hodlr",
    )(
        in_hbm(order.reshape(ROWS)),
        in_hbm(weights),
        in_hbm(weights.reshape(ROWS // 128, 128)),
        in_hbm(coupling.reshape(4 * ROWS, CAP)),
        in_hbm(coupling),
        in_hbm(rhs),
        in_hbm(rhs.reshape(ROWS, 1, CAP)),
    )
    applied, answer = pl.pallas_call(
        finish_kernel,
        in_specs=[anywhere] + [whole] * 5,
        out_specs=[anywhere, anywhere],
        out_shape=results,
        scratch_shapes=[vmem(ROWS, CAP), sems(PARTS)],
        compiler_params=pltpu.CompilerParams(vmem_limit_bytes=16 * 2**20),
        name="finish",
    )(*state)
    return applied.reshape(ROWS, 4, CAP), answer


def solution(mesh):
    rows = ("leaf", "sub")
    return jax.shard_map(
        local,
        mesh=mesh,
        in_specs=(P(rows, None, None), P(rows), P(rows, None), P(rows, None)),
        out_specs=(P(rows, None, None), P(rows, None)),
        check_vma=False,
    )
```

```python
import jax
import jax.numpy as jnp
from jax import lax
from jax.experimental import pallas as pl
from jax.experimental.pallas import tpu as pltpu
from jax.sharding import PartitionSpec as P

MESH = pl.DeviceIdType.MESH
F32 = jnp.float32
BF = jnp.bfloat16
ROWS = 2048
CAP = 128
AGENTS = 524288
CHUNK = 256
EARLY = 1280
LATER = 6


def split(x):
    head = x.astype(BF)
    return head, (x - head.astype(F32)).astype(BF)


def dot3(a, b, contract=((1,), (0,))):
    def one(p, q):
        return lax.dot_general(p, q, (contract, ((), ())), preferred_element_type=F32)

    return one(a[0], b[0]) + (one(a[0], b[1]) + one(a[1], b[0]))


def dot_full(a, b):
    return jnp.dot(a, b, precision=lax.Precision.HIGHEST, preferred_element_type=F32)


def sub_bcast(v, i):
    return jnp.broadcast_to(v[i : i + 1, :], (8, 128))


def lane_bcast(v, j):
    return jnp.broadcast_to(v[:, j : j + 1], (8, 128))


def lane_full(v, j):
    return jnp.maximum(lane_bcast(v, j), -3e38)


def recip(x):
    r = pltpu.reciprocal(x, approx=True)
    return r * (2.0 - x * r)


def eliminate_panel(cols, rows, ahead, off, lane, sub):
    cols, ahead = list(cols), list(ahead)
    out = jnp.where(
        (lane >= off) & (lane < off + 8), jnp.where(lane - off == sub, 1.0, 0.0), rows
    )
    for i in range(0, 8, 2):
        ci, cj = cols[i], cols[i + 1]
        a, b = sub_bcast(ci, i), sub_bcast(cj, i)
        b2, c = sub_bcast(ci, i + 1), sub_bcast(cj, i + 1)
        inv_det = recip(a * c - b * b2)
        n0 = jnp.where(sub == i, -c, jnp.where(sub == i + 1, b2, ci * c - cj * b2))
        n1 = jnp.where(sub == i, b, jnp.where(sub == i + 1, -a, cj * a - ci * b))
        f0, f1 = n0 * inv_det, n1 * inv_det
        keep = (sub != i) & (sub != i + 1)

        def update(v):
            return jnp.where(keep, v, 0.0) - (f0 * sub_bcast(v, i) + f1 * sub_bcast(v, i + 1))

        for j in range(i + 2, 8):
            cols[j] = update(cols[j])
        out = update(out)
        ahead = [update(v) for v in ahead]
    return out, ahead


def rank8(v, cols, rows):
    t = [cols[j] * rows[j] for j in range(8)]
    return v - (((t[0] + t[1]) + (t[2] + t[3])) + ((t[4] + t[5]) + (t[6] + t[7])))


def invert(matrix, block=8):
    s = [matrix[8 * q : 8 * q + 8, :] for q in range(16)]
    lane = lax.broadcasted_iota(jnp.int32, (8, 128), 1)
    sub = lax.broadcasted_iota(jnp.int32, (8, 128), 0)
    for first in range(0, 16, block):
        cols = [lane_full(s[first], 8 * first + j) for j in range(8)]
        for k in range(block):
            off = 8 * (first + k)
            inside = (lane >= off) & (lane < off + 8)
            last = k == block - 1
            rows = s[first + k]
            ahead = [] if last else [lane_full(rows, off + 8 + j) for j in range(8)]
            u, ahead = eliminate_panel(cols, rows, ahead, off, lane, sub)
            us = [sub_bcast(u, j) for j in range(8)]
            if not last:
                v = s[first + k + 1]
                lead = [lane_bcast(v, off + j) for j in range(8)]
                cols = [
                    rank8(lane_bcast(v, off + 8 + j), lead, [sub_bcast(ahead[j], i) for i in range(8)])
                    for j in range(8)
                ]
                s[first + k + 1] = rank8(jnp.where(inside, 0.0, v), lead, us)
            far = range(block - 1) if last else [(k + 2 + m) % block for m in range(block - 2)]
            for t in far:
                v = s[first + t]
                lead = [lane_bcast(v, off + j) for j in range(8)]
                s[first + t] = rank8(jnp.where(inside, 0.0, v), lead, us)
            s[first + k] = u
        rest = [(first + block + m) % 16 for m in range(16 - block)]
        left = jnp.concatenate([s[q] for q in rest], axis=0)
        left_lane = lax.broadcasted_iota(jnp.int32, left.shape, 1)
        inside = (left_lane >= 8 * first) & (left_lane < 8 * (first + block))
        parts = [jnp.zeros((8, 128), F32)] * 16
        parts[first : first + block] = s[first : first + block]
        wide = jnp.concatenate(parts, axis=0)
        new = jnp.where(inside, 0.0, left) - dot_full(jnp.where(inside, left, 0.0), wide)
        for m, q in enumerate(rest):
            s[q] = new[8 * m : 8 * m + 8]
    return jnp.concatenate(s, axis=0)


def kernel(
    order_hbm, w_hbm, wv_hbm, coup_hbm, coup_rows_hbm, rhs_hbm, rhs_rows_hbm,
    applied_out, answer_out, a0h_out, a0l_out, p0h, p0l,
    order, w_s, w_v, coup, coup_rows, rhs, rhs_rows, in_sem, applied, answer, a0h, a0l, out_sem,
    xh, xl, wh, wl,
    ga, ra, rsa, pa, fa,
    gb, rb, rsb, pb, fb,
    gc, rc, rsc, pc, fc, fd,
    z1s, z1r, z1ps, z1pr, p2,
    z2s, z2r, z2ps, z2pr, p1,
    z4s, z4r, z4bs, z4br,
    ph, plo, mt,
    core_sem, rsa_sem, aga_sem, rsb_sem, agb_sem, rsc_sem, agc_sem, agd_sem, z_sem,
):
    leaf = lax.axis_index("leaf")
    x = lax.axis_index("sub")
    z, y, c = leaf // 8, (leaf // 2) % 4, leaf % 2
    me = x * 4 + y

    def device(px, py, pz, pc):
        return (pz * 8 + py * 2 + pc, px)

    plane = []
    for dx in range(4):
        for dy in range(4):
            if (dx, dy) != (0, 0):
                plane.append((abs(2 - dx) + abs(2 - dy), dx, dy))
    plane = [((x + dx) % 4, (y + dy) % 4) for _, dx, dy in sorted(plane)]
    core_id = device(x, y, z, 1 - c)
    plane_ids = [device(px, py, z, c) for px, py in plane]
    plane_q = [px * 4 + py for px, py in plane]

    def z_flip(bit):
        return device(x, y, z + bit - 2 * bit * ((z // bit) % 2), c)

    z_ids = [z_flip(1), z_flip(2), z_flip(4)]

    quarter = ROWS // 4
    loads = []
    for i in range(4):
        at, at4 = pl.ds(quarter * i, quarter), pl.ds(4 * quarter * i, 4 * quarter)
        loads.append(pltpu.make_async_copy(coup_hbm.at[at4], coup.at[at4], in_sem.at[i]))
        loads.append(pltpu.make_async_copy(rhs_hbm.at[at], rhs.at[at], in_sem.at[4 + i]))
    loads.append(pltpu.make_async_copy(coup_rows_hbm, coup_rows, in_sem.at[8]))
    loads.append(pltpu.make_async_copy(rhs_rows_hbm, rhs_rows, in_sem.at[9]))
    weight_load = pltpu.make_async_copy(wv_hbm, w_v, in_sem.at[10])
    weight_load.start()
    for copy in loads[:8]:
        copy.start()
    loads.append(pltpu.make_async_copy(order_hbm, order, in_sem.at[11]))
    loads.append(pltpu.make_async_copy(w_hbm, w_s, in_sem.at[12]))

    barrier = pltpu.get_barrier_semaphore()
    everyone = plane_ids + [core_id] + z_ids
    for d in everyone:
        pl.semaphore_signal(barrier, inc=1, device_id=d, device_id_type=MESH)

    def send(src, dst, sems, i, d):
        copy = pltpu.make_async_remote_copy(
            src_ref=src, dst_ref=dst, send_sem=sems.at[0, i], recv_sem=sems.at[1, i],
            device_id=d, device_id_type=MESH,
        )
        copy.start()
        return copy

    def wait(copies):
        for copy in copies:
            copy.wait()

    def scatter(src, dst, sems):
        return [send(src.at[q], dst.at[i], sems, i, d) for i, (q, d) in enumerate(zip(plane_q, plane_ids))]

    def gather(src, dst, sems):
        return [send(src, dst.at[me], sems, i, d) for i, d in enumerate(plane_ids)]

    weight_load.wait()
    weight_cols = jnp.concatenate([w_v[...], jnp.zeros((112, 128), F32)], axis=0).T
    for g in range(16):
        if g % 4 == 0:
            wait(loads[g // 2 : g // 2 + 2])
        r0 = 128 * g
        col = jnp.broadcast_to(weight_cols[:, g : g + 1], (128, 128))
        for k in range(4):
            j = 3 - k
            basis = coup[pl.ds(4 * r0 + k, 128, stride=4), :]
            h, l = split(basis)
            xh[r0 : r0 + 128, 128 * j : 128 * j + 128] = h
            xl[r0 : r0 + 128, 128 * j : 128 * j + 128] = l
            h, l = split(basis * col)
            wh[r0 : r0 + 128, 128 * j : 128 * j + 128] = h
            wl[r0 : r0 + 128, 128 * j : 128 * j + 128] = l
        h, l = split(rhs[r0 : r0 + 128, :])
        xh[r0 : r0 + 128, 512:640] = h
        xl[r0 : r0 + 128, 512:640] = l

    for copy in loads[8:]:
        copy.start()

    def gram(a0, a1, b0, b1):
        return dot3(
            (wh[:, a0:a1], wl[:, a0:a1]), (xh[:, b0:b1], xl[:, b0:b1]), ((0,), (0,))
        )

    def pieces(value):
        return value.reshape(16, 8, 128)

    def put(ref, first, value):
        for k in range(value.shape[1] // 128):
            ref[:, first + k] = pieces(value[:, 128 * k : 128 * k + 128])

    put(ga, 0, gram(0, 128, 0, 256))
    pl.semaphore_wait(barrier, len(everyone))
    core_a = send(ga, ra, core_sem, 0, core_id)
    put(gb, 0, gram(0, 128, 256, 640))
    core_a.wait()
    ga[...] = ga[...] + ra[...]
    rs_a = scatter(ga, rsa, rsa_sem)
    put(gb, 3, gram(128, 256, 128, 256))
    core_b = send(gb, rb, core_sem, 1, core_id)
    m = gram(128, 256, 256, 640)
    for k in range(3):
        gc[0, :, k] = pieces(m[:, 128 * k : 128 * k + 128])
    core_b.wait()
    gb[...] = gb[...] + rb[...]
    rs_b = scatter(gb, rsb, rsb_sem)
    m = gram(256, 512, 256, 640)
    gc[0, :, 3] = pieces(m[:128, :128])
    gc[1, :, 0] = pieces(m[:128, 128:256])
    gc[1, :, 1] = pieces(m[:128, 256:])
    gc[1, :, 2] = pieces(m[128:, 128:256])
    gc[1, :, 3] = pieces(m[128:, 256:])
    core_c = send(gc.at[1 - c], rc, core_sem, 2, core_id)
    wait(rs_a)
    pa[...] = ga[me] + jnp.sum(rsa[...], axis=0)
    fa[me] = pa[...]
    ag_a = gather(pa, fa, aga_sem)
    core_c.wait()
    rc[...] = rc[...] + gc[c]
    rs_c = scatter(rc, rsc, rsc_sem)
    wait(rs_b)
    pb[...] = gb[me] + jnp.sum(rsb[...], axis=0)
    fb[me] = pb[...]
    ag_b = gather(pb, fb, agb_sem)

    wait(loads[8:])

    def permute(t, carry):
        for u in range(8):
            i = t * 8 + u
            r = order[i]
            s = w_s[r]
            applied[pl.ds(pl.multiple_of(4 * i, 4), 4), :] = coup_rows[r] * s
            answer[pl.ds(i, 1), :] = rhs_rows[r] * s
        return carry

    lax.fori_loop(0, EARLY // 8, permute, 0)

    eye = jnp.where(
        lax.broadcasted_iota(jnp.int32, (128, 128), 0)
        == lax.broadcasted_iota(jnp.int32, (128, 128), 1),
        1.0,
        0.0,
    )

    def block(ref, k):
        return ref[:, k].reshape(128, 128)

    def blocks(ref, first, count):
        return jnp.concatenate([block(ref, first + k) for k in range(count)], axis=1)

    def inverse_of(lead, nodes):
        scale = nodes / AGENTS
        return invert(eye + lead * scale) * scale

    def offset(level):
        return sum(128 * (k + 1) for k in range(3, level, -1))

    def keep(level, p):
        h, l = split(p)
        ph[:, offset(level) : offset(level) + p.shape[1]] = h
        plo[:, offset(level) : offset(level) + p.shape[1]] = l

    def subtract(level, start=0, end=ROWS // CHUNK):
        cut = slice(offset(level), offset(level) + 128 * (level + 1))

        def body(t, carry):
            r0 = pl.multiple_of(t * CHUNK, CHUNK)
            lead = split(applied[pl.ds(4 * r0 + level, CHUNK, stride=4), :])
            change = dot3(lead, (ph[:, cut], plo[:, cut]))
            for k in range(level):
                at = pl.ds(4 * r0 + level - 1 - k, CHUNK, stride=4)
                applied[at, :] = applied[at, :] - change[:, 128 * k : 128 * k + 128]
            at = pl.ds(r0, CHUNK)
            answer[at, :] = answer[at, :] - change[:, 128 * level :]
            return carry

        lax.fori_loop(start, end, body, 0)

    def turn(ref, first, count):
        for k in range(count):
            mt[128 * k : 128 * k + 128, :] = block(ref, first + k).T

    def reduced(inverse, count, lead, rest):
        own = [mt[pl.ds(pl.multiple_of(128 * k + 8 * me, 8), 8), :] for k in range(count)]
        left = dot_full(jnp.concatenate([mt[0:128, :]] + own, axis=0), inverse)
        return dot_full(left[:128], lead), dot_full(left[128:], rest)

    wait(ag_a)
    turn(fa, 1, 1)
    wait(rs_c)
    pc[c] = rc[me] + jnp.sum(rsc[...], axis=0)
    core_p = send(pc.at[c], pc.at[c], core_sem, 3, core_id)
    inverse = inverse_of(block(fa, 0), 8.0)
    wait(ag_b)
    for k in range(2):
        mt[128 * k + 128 : 128 * k + 256, :] = block(fb, k).T
    m32 = block(fa, 1)
    rest = blocks(fb, 0, 3)
    full, part = reduced(inverse, 3, m32, rest)
    core_p.wait()
    where = [(0, 0), (0, 1), (0, 2), (1, 0), (1, 1), (1, 2), (2, 1), (2, 2)]
    for k, (i, j) in enumerate(where):
        z1ps[k] = pc[k // 4, k % 4] - part[8 * i : 8 * i + 8, 128 * j : 128 * j + 128]
    z1p = send(z1ps, z1pr, z_sem, 1, z_ids[0])
    z1s[...] = block(fb, 3) - full
    z1 = send(z1s, z1r, z_sem, 0, z_ids[0])
    keep(3, dot_full(inverse, jnp.concatenate([m32, rest], axis=1)))
    lax.fori_loop(EARLY // 8, ROWS // 8, permute, 0)
    z1p.wait()
    p2[...] = z1ps[...] + z1pr[...]
    fc[me] = p2[0:4]
    ag_c = gather(p2.at[0:4], fc, agc_sem)

    z1.wait()
    inverse = inverse_of(z1s[...] + z1r[...], 4.0)
    subtract(3, 0, LATER)
    wait(ag_c)
    turn(fc, 0, 2)
    m21 = block(fc, 0)
    rest = blocks(fc, 1, 2)
    full, part = reduced(inverse, 2, m21, rest)
    for k, (i, j) in enumerate([(0, 0), (0, 1), (1, 0), (1, 1)]):
        z2ps[k] = p2[4 + k] - part[8 * i : 8 * i + 8, 128 * j : 128 * j + 128]
    z2p = send(z2ps, z2pr, z_sem, 3, z_ids[1])
    z2s[...] = block(fc, 3) - full
    z2 = send(z2s, z2r, z_sem, 2, z_ids[1])
    keep(2, dot_full(inverse, jnp.concatenate([m21, rest], axis=1)))
    subtract(3, LATER)
    subtract(2, 0, LATER)
    z2p.wait()
    p1[...] = z2ps[...] + z2pr[...]
    fd[me] = p1[...]
    ag_d = gather(p1, fd, agd_sem)

    z2.wait()
    inverse = inverse_of(z2s[...] + z2r[...], 2.0)
    subtract(2, LATER)
    wait(ag_d)
    turn(fd, 0, 1)
    m1 = blocks(fd, 0, 2)
    m0 = blocks(fd, 2, 2) - dot_full(dot_full(mt[0:128, :], inverse), m1)
    z4s[...] = m0[:, :128]
    z4 = send(z4s, z4r, z_sem, 4, z_ids[2])
    z4bs[...] = m0[:, 128:]
    z4b = send(z4bs, z4br, z_sem, 5, z_ids[2])
    keep(1, dot_full(inverse, m1))
    subtract(1)
    h, l = split(applied[pl.ds(0, ROWS, stride=4), :])
    a0h[...] = h
    a0l[...] = l
    outs = [
        pltpu.make_async_copy(a, b, out_sem.at[i])
        for i, (a, b) in enumerate(
            [(applied, applied_out), (answer, answer_out), (a0h, a0h_out), (a0l, a0l_out)]
        )
    ]
    for copy in outs:
        copy.start()

    z4.wait()
    inverse = inverse_of(z4s[...] + z4r[...], 1.0)
    z4b.wait()
    h, l = split(dot_full(inverse, z4bs[...] + z4br[...]))
    p0h[...] = h
    p0l[...] = l
    wait(outs)


PARTS = 8


def finish_kernel(applied_in, answer_in, a0h, a0l, p0h, p0l, applied_out, answer_out, ans, sem):
    rows = ROWS // PARTS
    outs = []
    for i in range(PARTS):
        at4 = pl.ds(4 * rows * i, 4 * rows)
        outs.append(pltpu.make_async_copy(applied_in.at[at4], applied_out.at[at4], sem.at[0, i]))
        outs[-1].start()
    for i in range(PARTS):
        at = pl.ds(rows * i, rows)
        ans[at, :] = answer_in[at, :] - dot3((a0h[at, :], a0l[at, :]), (p0h[...], p0l[...]))
        outs.append(pltpu.make_async_copy(ans.at[at], answer_out.at[at], sem.at[1, i]))
        outs[-1].start()
    for copy in outs:
        copy.wait()


def local(coupling, weights, rhs, order):
    def vmem(*shape, dtype=F32):
        return pltpu.VMEM(shape, dtype)

    def sems(n):
        return pltpu.SemaphoreType.DMA((2, n))

    whole = pl.BlockSpec(memory_space=pltpu.VMEM)
    anywhere = pl.BlockSpec(memory_space=pl.ANY)
    results = [
        jax.ShapeDtypeStruct((4 * ROWS, CAP), F32),
        jax.ShapeDtypeStruct((ROWS, CAP), F32),
    ]
    last = [jax.ShapeDtypeStruct((ROWS, CAP), BF)] * 2 + [jax.ShapeDtypeStruct((CAP, CAP), BF)] * 2

    def in_hbm(v):
        return pltpu.with_memory_space_constraint(v, pltpu.HBM)

    state = pl.pallas_call(
        kernel,
        in_specs=[anywhere] * 7,
        out_specs=[anywhere] * 4 + [whole] * 2,
        out_shape=results + last,
        scratch_shapes=[
            pltpu.SMEM((ROWS,), jnp.int32), pltpu.SMEM((ROWS,), F32), vmem(16, CAP),
            vmem(4 * ROWS, CAP), vmem(ROWS, 4, CAP), vmem(ROWS, CAP), vmem(ROWS, 1, CAP),
            pltpu.SemaphoreType.DMA((13,)),
            vmem(4 * ROWS, CAP), vmem(ROWS, CAP), vmem(ROWS, CAP, dtype=BF), vmem(ROWS, CAP, dtype=BF),
            pltpu.SemaphoreType.DMA((4,)),
            vmem(ROWS, 640, dtype=BF), vmem(ROWS, 640, dtype=BF),
            vmem(ROWS, 512, dtype=BF), vmem(ROWS, 512, dtype=BF),
            vmem(16, 2, 8, 128), vmem(16, 2, 8, 128), vmem(15, 2, 8, 128), vmem(2, 8, 128), vmem(16, 2, 8, 128),
            vmem(16, 4, 8, 128), vmem(16, 4, 8, 128), vmem(15, 4, 8, 128), vmem(4, 8, 128), vmem(16, 4, 8, 128),
            vmem(2, 16, 4, 8, 128), vmem(16, 4, 8, 128), vmem(15, 4, 8, 128), vmem(2, 4, 8, 128),
            vmem(16, 4, 8, 128), vmem(16, 4, 8, 128),
            vmem(128, 128), vmem(128, 128), vmem(8, 8, 128), vmem(8, 8, 128), vmem(8, 8, 128),
            vmem(128, 128), vmem(128, 128), vmem(4, 8, 128), vmem(4, 8, 128), vmem(4, 8, 128),
            vmem(128, 128), vmem(128, 128), vmem(128, 128), vmem(128, 128),
            vmem(128, 1280, dtype=BF), vmem(128, 1280, dtype=BF), vmem(384, 128),
            sems(4), sems(15), sems(15), sems(15), sems(15), sems(15), sems(15), sems(15), sems(6),
        ],
        compiler_params=pltpu.CompilerParams(
            collective_id=0, has_side_effects=True, vmem_limit_bytes=44 * 2**20
        ),
        name="hodlr",
    )(
        in_hbm(order.reshape(ROWS)),
        in_hbm(weights),
        in_hbm(weights.reshape(ROWS // 128, 128)),
        in_hbm(coupling.reshape(4 * ROWS, CAP)),
        in_hbm(coupling),
        in_hbm(rhs),
        in_hbm(rhs.reshape(ROWS, 1, CAP)),
    )
    applied, answer = pl.pallas_call(
        finish_kernel,
        in_specs=[anywhere] + [whole] * 5,
        out_specs=[anywhere, anywhere],
        out_shape=results,
        scratch_shapes=[vmem(ROWS, CAP), sems(PARTS)],
        compiler_params=pltpu.CompilerParams(vmem_limit_bytes=16 * 2**20),
        name="finish",
    )(*state)
    return applied.reshape(ROWS, 4, CAP), answer


def solution(mesh):
    rows = ("leaf", "sub")
    return jax.shard_map(
        local,
        mesh=mesh,
        in_specs=(P(rows, None, None), P(rows), P(rows, None), P(rows, None)),
        out_specs=(P(rows, None, None), P(rows, None)),
        check_vma=False,
    )
```

```python
import jax
import jax.numpy as jnp
from jax import lax
from jax.experimental import pallas as pl
from jax.experimental.pallas import tpu as pltpu
from jax.sharding import PartitionSpec as P

MESH = pl.DeviceIdType.MESH
F32 = jnp.float32
BF = jnp.bfloat16
ROWS = 2048
CAP = 128
AGENTS = 524288
CHUNK = 256
EARLY = 1280
LATER = 6


def split(x):
    head = x.astype(BF)
    return head, (x - head.astype(F32)).astype(BF)


def dot3(a, b, contract=((1,), (0,))):
    def one(p, q):
        return lax.dot_general(p, q, (contract, ((), ())), preferred_element_type=F32)

    return one(a[0], b[0]) + (one(a[0], b[1]) + one(a[1], b[0]))


def dot_full(a, b):
    return jnp.dot(a, b, precision=lax.Precision.HIGHEST, preferred_element_type=F32)


def sub_bcast(v, i):
    return jnp.broadcast_to(v[i : i + 1, :], (8, 128))


def lane_bcast(v, j):
    return jnp.broadcast_to(v[:, j : j + 1], (8, 128))


def lane_full(v, j):
    return jnp.maximum(lane_bcast(v, j), -3e38)


def recip(x):
    r = pltpu.reciprocal(x, approx=True)
    return r * (2.0 - x * r)


def eliminate_panel(cols, rows, ahead, off, lane, sub):
    cols, ahead = list(cols), list(ahead)
    out = jnp.where(
        (lane >= off) & (lane < off + 8), jnp.where(lane - off == sub, 1.0, 0.0), rows
    )
    for i in range(0, 8, 2):
        ci, cj = cols[i], cols[i + 1]
        a, b = sub_bcast(ci, i), sub_bcast(cj, i)
        b2, c = sub_bcast(ci, i + 1), sub_bcast(cj, i + 1)
        inv_det = recip(a * c - b * b2)
        n0 = jnp.where(sub == i, -c, jnp.where(sub == i + 1, b2, ci * c - cj * b2))
        n1 = jnp.where(sub == i, b, jnp.where(sub == i + 1, -a, cj * a - ci * b))
        f0, f1 = n0 * inv_det, n1 * inv_det
        keep = (sub != i) & (sub != i + 1)

        def update(v):
            return jnp.where(keep, v, 0.0) - (f0 * sub_bcast(v, i) + f1 * sub_bcast(v, i + 1))

        for j in range(i + 2, 8):
            cols[j] = update(cols[j])
        out = update(out)
        ahead = [update(v) for v in ahead]
    return out, ahead


def rank8(v, cols, rows):
    t = [cols[j] * rows[j] for j in range(8)]
    return v - (((t[0] + t[1]) + (t[2] + t[3])) + ((t[4] + t[5]) + (t[6] + t[7])))


def invert(matrix, block=8):
    s = [matrix[8 * q : 8 * q + 8, :] for q in range(16)]
    lane = lax.broadcasted_iota(jnp.int32, (8, 128), 1)
    sub = lax.broadcasted_iota(jnp.int32, (8, 128), 0)
    for first in range(0, 16, block):
        cols = [lane_full(s[first], 8 * first + j) for j in range(8)]
        for k in range(block):
            off = 8 * (first + k)
            inside = (lane >= off) & (lane < off + 8)
            last = k == block - 1
            rows = s[first + k]
            ahead = [] if last else [lane_full(rows, off + 8 + j) for j in range(8)]
            u, ahead = eliminate_panel(cols, rows, ahead, off, lane, sub)
            us = [sub_bcast(u, j) for j in range(8)]
            if not last:
                v = s[first + k + 1]
                lead = [lane_bcast(v, off + j) for j in range(8)]
                cols = [
                    rank8(lane_bcast(v, off + 8 + j), lead, [sub_bcast(ahead[j], i) for i in range(8)])
                    for j in range(8)
                ]
                s[first + k + 1] = rank8(jnp.where(inside, 0.0, v), lead, us)
            far = range(block - 1) if last else [(k + 2 + m) % block for m in range(block - 2)]
            for t in far:
                v = s[first + t]
                lead = [lane_bcast(v, off + j) for j in range(8)]
                s[first + t] = rank8(jnp.where(inside, 0.0, v), lead, us)
            s[first + k] = u
        rest = [(first + block + m) % 16 for m in range(16 - block)]
        left = jnp.concatenate([s[q] for q in rest], axis=0)
        left_lane = lax.broadcasted_iota(jnp.int32, left.shape, 1)
        inside = (left_lane >= 8 * first) & (left_lane < 8 * (first + block))
        parts = [jnp.zeros((8, 128), F32)] * 16
        parts[first : first + block] = s[first : first + block]
        wide = jnp.concatenate(parts, axis=0)
        new = jnp.where(inside, 0.0, left) - dot_full(jnp.where(inside, left, 0.0), wide)
        for m, q in enumerate(rest):
            s[q] = new[8 * m : 8 * m + 8]
    return jnp.concatenate(s, axis=0)


def kernel(
    order_hbm, w_hbm, wv_hbm, coup_hbm, coup_rows_hbm, rhs_hbm, rhs_rows_hbm,
    applied_out, answer_out, lead_out, p0,
    order, w_s, w_v, coup, coup_rows, rhs, rhs_rows, in_sem, applied, answer, lead, out_sem,
    xh, xl, wh, wl,
    ga, ra, rsa, pa, fa,
    gb, rb, rsb, pb, fb,
    gc, rc, rsc, pc, fc, fd,
    z1s, z1r, z1ps, z1pr, p2,
    z2s, z2r, z2ps, z2pr, p1,
    z4s, z4r, z4bs, z4br,
    ph, plo, mt,
    core_sem, rsa_sem, aga_sem, rsb_sem, agb_sem, rsc_sem, agc_sem, agd_sem, z_sem,
):
    leaf = lax.axis_index("leaf")
    x = lax.axis_index("sub")
    z, y, c = leaf // 8, (leaf // 2) % 4, leaf % 2
    me = x * 4 + y

    def device(px, py, pz, pc):
        return (pz * 8 + py * 2 + pc, px)

    plane = []
    for dx in range(4):
        for dy in range(4):
            if (dx, dy) != (0, 0):
                plane.append((abs(2 - dx) + abs(2 - dy), dx, dy))
    plane = [((x + dx) % 4, (y + dy) % 4) for _, dx, dy in sorted(plane)]
    core_id = device(x, y, z, 1 - c)
    plane_ids = [device(px, py, z, c) for px, py in plane]
    plane_q = [px * 4 + py for px, py in plane]

    def z_flip(bit):
        return device(x, y, z + bit - 2 * bit * ((z // bit) % 2), c)

    z_ids = [z_flip(1), z_flip(2), device(x, y, 7 - z, c)]

    quarter = ROWS // 4
    loads = []
    for i in range(4):
        at, at4 = pl.ds(quarter * i, quarter), pl.ds(4 * quarter * i, 4 * quarter)
        loads.append(pltpu.make_async_copy(coup_hbm.at[at4], coup.at[at4], in_sem.at[i]))
        loads.append(pltpu.make_async_copy(rhs_hbm.at[at], rhs.at[at], in_sem.at[4 + i]))
    loads.append(pltpu.make_async_copy(coup_rows_hbm, coup_rows, in_sem.at[8]))
    loads.append(pltpu.make_async_copy(rhs_rows_hbm, rhs_rows, in_sem.at[9]))
    weight_load = pltpu.make_async_copy(wv_hbm, w_v, in_sem.at[10])
    weight_load.start()
    for copy in loads[:8]:
        copy.start()
    loads.append(pltpu.make_async_copy(order_hbm, order, in_sem.at[11]))
    loads.append(pltpu.make_async_copy(w_hbm, w_s, in_sem.at[12]))

    barrier = pltpu.get_barrier_semaphore()
    everyone = plane_ids + [core_id] + z_ids
    for d in everyone:
        pl.semaphore_signal(barrier, inc=1, device_id=d, device_id_type=MESH)

    def send(src, dst, sems, i, d):
        copy = pltpu.make_async_remote_copy(
            src_ref=src, dst_ref=dst, send_sem=sems.at[0, i], recv_sem=sems.at[1, i],
            device_id=d, device_id_type=MESH,
        )
        copy.start()
        return copy

    def wait(copies):
        for copy in copies:
            copy.wait()

    def scatter(src, dst, sems):
        return [send(src.at[q], dst.at[i], sems, i, d) for i, (q, d) in enumerate(zip(plane_q, plane_ids))]

    def gather(src, dst, sems):
        return [send(src, dst.at[me], sems, i, d) for i, d in enumerate(plane_ids)]

    weight_load.wait()
    weight_cols = jnp.concatenate([w_v[...], jnp.zeros((112, 128), F32)], axis=0).T
    for g in range(16):
        if g % 4 == 0:
            wait(loads[g // 2 : g // 2 + 2])
        r0 = 128 * g
        col = jnp.broadcast_to(weight_cols[:, g : g + 1], (128, 128))
        for k in range(4):
            j = 3 - k
            basis = coup[pl.ds(4 * r0 + k, 128, stride=4), :]
            h, l = split(basis)
            xh[r0 : r0 + 128, 128 * j : 128 * j + 128] = h
            xl[r0 : r0 + 128, 128 * j : 128 * j + 128] = l
            h, l = split(basis * col)
            wh[r0 : r0 + 128, 128 * j : 128 * j + 128] = h
            wl[r0 : r0 + 128, 128 * j : 128 * j + 128] = l
        h, l = split(rhs[r0 : r0 + 128, :])
        xh[r0 : r0 + 128, 512:640] = h
        xl[r0 : r0 + 128, 512:640] = l

    for copy in loads[8:]:
        copy.start()

    def gram(a0, a1, b0, b1):
        return dot3(
            (wh[:, a0:a1], wl[:, a0:a1]), (xh[:, b0:b1], xl[:, b0:b1]), ((0,), (0,))
        )

    def pieces(value):
        return value.reshape(16, 8, 128)

    def put(ref, first, value):
        for k in range(value.shape[1] // 128):
            ref[:, first + k] = pieces(value[:, 128 * k : 128 * k + 128])

    put(ga, 0, gram(0, 128, 0, 256))
    pl.semaphore_wait(barrier, len(everyone))
    core_a = send(ga, ra, core_sem, 0, core_id)
    put(gb, 0, gram(0, 128, 256, 640))
    core_a.wait()
    ga[...] = ga[...] + ra[...]
    rs_a = scatter(ga, rsa, rsa_sem)
    put(gb, 3, gram(128, 256, 128, 256))
    core_b = send(gb, rb, core_sem, 1, core_id)
    m = gram(128, 256, 256, 640)
    for k in range(3):
        gc[0, :, k] = pieces(m[:, 128 * k : 128 * k + 128])
    core_b.wait()
    gb[...] = gb[...] + rb[...]
    rs_b = scatter(gb, rsb, rsb_sem)
    m = gram(256, 384, 256, 640)
    gc[0, :, 3] = pieces(m[:, :128])
    gc[1, :, 0] = pieces(m[:, 128:256])
    gc[1, :, 1] = pieces(m[:, 256:])
    m = gram(384, 512, 384, 640)
    gc[1, :, 2] = pieces(m[:, :128])
    gc[1, :, 3] = pieces(m[:, 128:])
    core_c = send(gc.at[1 - c], rc, core_sem, 2, core_id)
    wait(rs_a)
    pa[...] = ga[me] + jnp.sum(rsa[...], axis=0)
    fa[me] = pa[...]
    ag_a = gather(pa, fa, aga_sem)
    core_c.wait()
    rc[...] = rc[...] + gc[c]
    rs_c = scatter(rc, rsc, rsc_sem)
    wait(rs_b)
    pb[...] = gb[me] + jnp.sum(rsb[...], axis=0)
    fb[me] = pb[...]
    ag_b = gather(pb, fb, agb_sem)

    wait(loads[8:])

    def permute(t, carry):
        for u in range(8):
            i = t * 8 + u
            r = order[i]
            s = w_s[r]
            applied[pl.ds(pl.multiple_of(4 * i, 4), 4), :] = coup_rows[r] * s
            answer[pl.ds(i, 1), :] = rhs_rows[r] * s
        return carry

    lax.fori_loop(0, EARLY // 8, permute, 0)

    eye = jnp.where(
        lax.broadcasted_iota(jnp.int32, (128, 128), 0)
        == lax.broadcasted_iota(jnp.int32, (128, 128), 1),
        1.0,
        0.0,
    )

    def block(ref, k):
        return ref[:, k].reshape(128, 128)

    def blocks(ref, first, count):
        return jnp.concatenate([block(ref, first + k) for k in range(count)], axis=1)

    def inverse_of(lead, nodes):
        scale = nodes / AGENTS
        return invert(eye + lead * scale) * scale

    def offset(level):
        return sum(128 * (k + 1) for k in range(3, level, -1))

    def keep(level, p):
        h, l = split(p)
        ph[:, offset(level) : offset(level) + p.shape[1]] = h
        plo[:, offset(level) : offset(level) + p.shape[1]] = l

    def subtract(level, start=0, end=ROWS // CHUNK):
        cut = slice(offset(level), offset(level) + 128 * (level + 1))

        def body(t, carry):
            r0 = pl.multiple_of(t * CHUNK, CHUNK)
            lead = split(applied[pl.ds(4 * r0 + level, CHUNK, stride=4), :])
            change = dot3(lead, (ph[:, cut], plo[:, cut]))
            for k in range(level):
                at = pl.ds(4 * r0 + level - 1 - k, CHUNK, stride=4)
                applied[at, :] = applied[at, :] - change[:, 128 * k : 128 * k + 128]
            at = pl.ds(r0, CHUNK)
            answer[at, :] = answer[at, :] - change[:, 128 * level :]
            return carry

        lax.fori_loop(start, end, body, 0)

    def turn(ref, first, count):
        for k in range(count):
            mt[128 * k : 128 * k + 128, :] = block(ref, first + k).T

    def reduced(inverse, count, lead, rest):
        own = [mt[pl.ds(pl.multiple_of(128 * k + 8 * me, 8), 8), :] for k in range(count)]
        left = dot_full(jnp.concatenate([mt[0:128, :]] + own, axis=0), inverse)
        return dot_full(left[:128], lead), dot_full(left[128:], rest)

    wait(ag_a)
    turn(fa, 1, 1)
    wait(rs_c)
    pc[c] = rc[me] + jnp.sum(rsc[...], axis=0)
    core_p = send(pc.at[c], pc.at[c], core_sem, 3, core_id)
    inverse = inverse_of(block(fa, 0), 8.0)
    wait(ag_b)
    for k in range(2):
        mt[128 * k + 128 : 128 * k + 256, :] = block(fb, k).T
    m32 = block(fa, 1)
    rest = blocks(fb, 0, 3)
    full, part = reduced(inverse, 3, m32, rest)
    core_p.wait()
    where = [(0, 0), (0, 1), (0, 2), (1, 0), (1, 1), (1, 2), (2, 1), (2, 2)]
    for k, (i, j) in enumerate(where):
        z1ps[k] = pc[k // 4, k % 4] - part[8 * i : 8 * i + 8, 128 * j : 128 * j + 128]
    z1p = send(z1ps, z1pr, z_sem, 1, z_ids[0])
    z1s[...] = block(fb, 3) - full
    z1 = send(z1s, z1r, z_sem, 0, z_ids[0])
    keep(3, dot_full(inverse, jnp.concatenate([m32, rest], axis=1)))
    lax.fori_loop(EARLY // 8, ROWS // 8, permute, 0)
    z1p.wait()
    p2[...] = z1ps[...] + z1pr[...]
    fc[me] = p2[0:4]
    ag_c = gather(p2.at[0:4], fc, agc_sem)

    z1.wait()
    inverse = inverse_of(z1s[...] + z1r[...], 4.0)
    subtract(3, 0, LATER)
    wait(ag_c)
    turn(fc, 0, 2)
    m21 = block(fc, 0)
    rest = blocks(fc, 1, 2)
    full, part = reduced(inverse, 2, m21, rest)
    for k, (i, j) in enumerate([(0, 0), (0, 1), (1, 0), (1, 1)]):
        z2ps[k] = p2[4 + k] - part[8 * i : 8 * i + 8, 128 * j : 128 * j + 128]
    z2p = send(z2ps, z2pr, z_sem, 3, z_ids[1])
    z2s[...] = block(fc, 3) - full
    z2 = send(z2s, z2r, z_sem, 2, z_ids[1])
    keep(2, dot_full(inverse, jnp.concatenate([m21, rest], axis=1)))
    subtract(3, LATER)
    subtract(2, 0, LATER)
    z2p.wait()
    p1[...] = z2ps[...] + z2pr[...]
    fd[me] = p1[...]
    ag_d = gather(p1, fd, agd_sem)

    z2.wait()
    inverse = inverse_of(z2s[...] + z2r[...], 2.0)
    subtract(2, LATER)
    wait(ag_d)
    turn(fd, 0, 1)
    m1 = blocks(fd, 0, 2)
    left = dot_full(mt[0:128, :], inverse)
    z4s[...] = block(fd, 2) - dot_full(left, m1[:, :128])
    z4 = send(z4s, z4r, z_sem, 4, z_ids[2])
    z4bs[...] = block(fd, 3) - dot_full(left, m1[:, 128:])
    z4b = send(z4bs, z4br, z_sem, 5, z_ids[2])
    keep(1, dot_full(inverse, m1))
    subtract(1)
    h, l = split(applied[pl.ds(0, ROWS, stride=4), :])
    lead[:, :128] = h
    lead[:, 128:] = l
    outs = [
        pltpu.make_async_copy(a, b, out_sem.at[i])
        for i, (a, b) in enumerate(
            [(applied, applied_out), (answer, answer_out), (lead, lead_out)]
        )
    ]
    for copy in outs:
        copy.start()

    z4.wait()
    inverse = inverse_of(z4s[...] + z4r[...], 1.0)
    z4b.wait()
    h, l = split(dot_full(inverse, z4bs[...] + z4br[...]))
    p0[:128, :128] = h
    p0[:128, 128:] = l
    p0[128:, :128] = h
    p0[128:, 128:] = jnp.zeros((128, 128), BF)
    wait(outs)


PARTS = 8


def finish_kernel(applied_in, answer_in, lead, p0, applied_out, answer_out, ans, sem):
    rows = ROWS // PARTS
    outs = []
    for i in range(PARTS):
        at4 = pl.ds(4 * rows * i, 4 * rows)
        outs.append(pltpu.make_async_copy(applied_in.at[at4], applied_out.at[at4], sem.at[0, i]))
        outs[-1].start()
    for i in range(PARTS):
        at = pl.ds(rows * i, rows)
        change = jnp.dot(lead[at, :], p0[...], preferred_element_type=F32)
        ans[at, :] = answer_in[at, :] - (change[:, :128] + change[:, 128:])
        outs.append(pltpu.make_async_copy(ans.at[at], answer_out.at[at], sem.at[1, i]))
        outs[-1].start()
    for copy in outs:
        copy.wait()


def local(coupling, weights, rhs, order):
    def vmem(*shape, dtype=F32):
        return pltpu.VMEM(shape, dtype)

    def sems(n):
        return pltpu.SemaphoreType.DMA((2, n))

    whole = pl.BlockSpec(memory_space=pltpu.VMEM)
    anywhere = pl.BlockSpec(memory_space=pl.ANY)
    results = [
        jax.ShapeDtypeStruct((4 * ROWS, CAP), F32),
        jax.ShapeDtypeStruct((ROWS, CAP), F32),
    ]
    last = [jax.ShapeDtypeStruct((ROWS, 2 * CAP), BF), jax.ShapeDtypeStruct((2 * CAP, 2 * CAP), BF)]

    def in_hbm(v):
        return pltpu.with_memory_space_constraint(v, pltpu.HBM)

    state = pl.pallas_call(
        kernel,
        in_specs=[anywhere] * 7,
        out_specs=[anywhere] * 3 + [whole],
        out_shape=results + last,
        scratch_shapes=[
            pltpu.SMEM((ROWS,), jnp.int32), pltpu.SMEM((ROWS,), F32), vmem(16, CAP),
            vmem(4 * ROWS, CAP), vmem(ROWS, 4, CAP), vmem(ROWS, CAP), vmem(ROWS, 1, CAP),
            pltpu.SemaphoreType.DMA((13,)),
            vmem(4 * ROWS, CAP), vmem(ROWS, CAP), vmem(ROWS, 2 * CAP, dtype=BF),
            pltpu.SemaphoreType.DMA((3,)),
            vmem(ROWS, 640, dtype=BF), vmem(ROWS, 640, dtype=BF),
            vmem(ROWS, 512, dtype=BF), vmem(ROWS, 512, dtype=BF),
            vmem(16, 2, 8, 128), vmem(16, 2, 8, 128), vmem(15, 2, 8, 128), vmem(2, 8, 128), vmem(16, 2, 8, 128),
            vmem(16, 4, 8, 128), vmem(16, 4, 8, 128), vmem(15, 4, 8, 128), vmem(4, 8, 128), vmem(16, 4, 8, 128),
            vmem(2, 16, 4, 8, 128), vmem(16, 4, 8, 128), vmem(15, 4, 8, 128), vmem(2, 4, 8, 128),
            vmem(16, 4, 8, 128), vmem(16, 4, 8, 128),
            vmem(128, 128), vmem(128, 128), vmem(8, 8, 128), vmem(8, 8, 128), vmem(8, 8, 128),
            vmem(128, 128), vmem(128, 128), vmem(4, 8, 128), vmem(4, 8, 128), vmem(4, 8, 128),
            vmem(128, 128), vmem(128, 128), vmem(128, 128), vmem(128, 128),
            vmem(128, 1280, dtype=BF), vmem(128, 1280, dtype=BF), vmem(384, 128),
            sems(4), sems(15), sems(15), sems(15), sems(15), sems(15), sems(15), sems(15), sems(6),
        ],
        compiler_params=pltpu.CompilerParams(
            collective_id=0, has_side_effects=True, vmem_limit_bytes=44 * 2**20
        ),
        name="hodlr",
    )(
        in_hbm(order.reshape(ROWS)),
        in_hbm(weights),
        in_hbm(weights.reshape(ROWS // 128, 128)),
        in_hbm(coupling.reshape(4 * ROWS, CAP)),
        in_hbm(coupling),
        in_hbm(rhs),
        in_hbm(rhs.reshape(ROWS, 1, CAP)),
    )
    applied, answer = pl.pallas_call(
        finish_kernel,
        in_specs=[anywhere] + [whole] * 3,
        out_specs=[anywhere, anywhere],
        out_shape=results,
        scratch_shapes=[vmem(ROWS, CAP), sems(PARTS)],
        compiler_params=pltpu.CompilerParams(vmem_limit_bytes=16 * 2**20),
        name="finish",
    )(*state)
    return applied.reshape(ROWS, 4, CAP), answer


def solution(mesh):
    rows = ("leaf", "sub")
    return jax.shard_map(
        local,
        mesh=mesh,
        in_specs=(P(rows, None, None), P(rows), P(rows, None), P(rows, None)),
        out_specs=(P(rows, None, None), P(rows, None)),
        check_vma=False,
    )
```

```python
import jax
import jax.numpy as jnp
from jax import lax
from jax.experimental import pallas as pl
from jax.experimental.pallas import tpu as pltpu
from jax.sharding import PartitionSpec as P

MESH = pl.DeviceIdType.MESH
F32 = jnp.float32
BF = jnp.bfloat16
ROWS = 2048
CAP = 128
AGENTS = 524288
CHUNK = 256
EARLY = 1280
LATER = 6


def split(x):
    head = x.astype(BF)
    return head, (x - head.astype(F32)).astype(BF)


def dot3(a, b, contract=((1,), (0,))):
    def one(p, q):
        return lax.dot_general(p, q, (contract, ((), ())), preferred_element_type=F32)

    return one(a[0], b[0]) + (one(a[0], b[1]) + one(a[1], b[0]))


def dot_full(a, b):
    return jnp.dot(a, b, precision=lax.Precision.HIGHEST, preferred_element_type=F32)


def sub_bcast(v, i):
    return jnp.broadcast_to(v[i : i + 1, :], (8, 128))


def lane_bcast(v, j):
    return jnp.broadcast_to(v[:, j : j + 1], (8, 128))


def lane_full(v, j):
    return jnp.maximum(lane_bcast(v, j), -3e38)


def recip(x):
    r = pltpu.reciprocal(x, approx=True)
    return r * (2.0 - x * r)


def eliminate_panel(cols, rows, ahead, off, lane, sub):
    cols, ahead = list(cols), list(ahead)
    out = jnp.where(
        (lane >= off) & (lane < off + 8), jnp.where(lane - off == sub, 1.0, 0.0), rows
    )
    for i in range(0, 8, 2):
        ci, cj = cols[i], cols[i + 1]
        a, b = sub_bcast(ci, i), sub_bcast(cj, i)
        b2, c = sub_bcast(ci, i + 1), sub_bcast(cj, i + 1)
        inv_det = recip(a * c - b * b2)
        n0 = jnp.where(sub == i, -c, jnp.where(sub == i + 1, b2, ci * c - cj * b2))
        n1 = jnp.where(sub == i, b, jnp.where(sub == i + 1, -a, cj * a - ci * b))
        f0, f1 = n0 * inv_det, n1 * inv_det
        keep = (sub != i) & (sub != i + 1)

        def update(v):
            return jnp.where(keep, v, 0.0) - (f0 * sub_bcast(v, i) + f1 * sub_bcast(v, i + 1))

        for j in range(i + 2, 8):
            cols[j] = update(cols[j])
        out = update(out)
        ahead = [update(v) for v in ahead]
    return out, ahead


def rank8(v, cols, rows):
    t = [cols[j] * rows[j] for j in range(8)]
    return v - (((t[0] + t[1]) + (t[2] + t[3])) + ((t[4] + t[5]) + (t[6] + t[7])))


def invert(matrix, block=8):
    s = [matrix[8 * q : 8 * q + 8, :] for q in range(16)]
    lane = lax.broadcasted_iota(jnp.int32, (8, 128), 1)
    sub = lax.broadcasted_iota(jnp.int32, (8, 128), 0)
    for first in range(0, 16, block):
        cols = [lane_full(s[first], 8 * first + j) for j in range(8)]
        for k in range(block):
            off = 8 * (first + k)
            inside = (lane >= off) & (lane < off + 8)
            last = k == block - 1
            rows = s[first + k]
            ahead = [] if last else [lane_full(rows, off + 8 + j) for j in range(8)]
            u, ahead = eliminate_panel(cols, rows, ahead, off, lane, sub)
            us = [sub_bcast(u, j) for j in range(8)]
            if not last:
                v = s[first + k + 1]
                lead = [lane_bcast(v, off + j) for j in range(8)]
                cols = [
                    rank8(lane_bcast(v, off + 8 + j), lead, [sub_bcast(ahead[j], i) for i in range(8)])
                    for j in range(8)
                ]
                s[first + k + 1] = rank8(jnp.where(inside, 0.0, v), lead, us)
            far = range(block - 1) if last else [(k + 2 + m) % block for m in range(block - 2)]
            for t in far:
                v = s[first + t]
                lead = [lane_bcast(v, off + j) for j in range(8)]
                s[first + t] = rank8(jnp.where(inside, 0.0, v), lead, us)
            s[first + k] = u
        rest = [(first + block + m) % 16 for m in range(16 - block)]
        left = jnp.concatenate([s[q] for q in rest], axis=0)
        left_lane = lax.broadcasted_iota(jnp.int32, left.shape, 1)
        inside = (left_lane >= 8 * first) & (left_lane < 8 * (first + block))
        parts = [jnp.zeros((8, 128), F32)] * 16
        parts[first : first + block] = s[first : first + block]
        wide = jnp.concatenate(parts, axis=0)
        new = jnp.where(inside, 0.0, left) - dot_full(jnp.where(inside, left, 0.0), wide)
        for m, q in enumerate(rest):
            s[q] = new[8 * m : 8 * m + 8]
    return jnp.concatenate(s, axis=0)


def kernel(
    order_hbm, w_hbm, wv_hbm, coup_hbm, coup_rows_hbm, rhs_hbm, rhs_rows_hbm,
    applied_out, answer_out, lead_out, p0,
    order, w_s, w_v, coup, coup_rows, rhs, rhs_rows, in_sem, applied, answer, lead, out_sem,
    xh, xl, wh, wl,
    ga, ra, rsa, pa, fa,
    gb, rb, rsb, pb, fb,
    gc, rc, rsc, pc, fc, fd,
    z1s, z1r, z1ps, z1pr, p2,
    z2s, z2r, z2ps, z2pr, p1,
    z4s, z4r, z4bs, z4br,
    ph, plo, mt,
    core_sem, rsa_sem, aga_sem, rsb_sem, agb_sem, rsc_sem, agc_sem, agd_sem, z_sem,
):
    leaf = lax.axis_index("leaf")
    x = lax.axis_index("sub")
    z, y, c = leaf // 8, (leaf // 2) % 4, leaf % 2
    me = x * 4 + y

    def device(px, py, pz, pc):
        return (pz * 8 + py * 2 + pc, px)

    plane = []
    for dx in range(4):
        for dy in range(4):
            if (dx, dy) != (0, 0):
                plane.append((abs(2 - dx) + abs(2 - dy), dx, dy))
    plane = [((x + dx) % 4, (y + dy) % 4) for _, dx, dy in sorted(plane)]
    core_id = device(x, y, z, 1 - c)
    plane_ids = [device(px, py, z, c) for px, py in plane]
    plane_q = [px * 4 + py for px, py in plane]

    def z_flip(bit):
        return device(x, y, z + bit - 2 * bit * ((z // bit) % 2), c)

    z_ids = [z_flip(1), z_flip(2), device(x, y, 7 - z, c)]

    quarter = ROWS // 4
    loads = []
    for i in range(4):
        at, at4 = pl.ds(quarter * i, quarter), pl.ds(4 * quarter * i, 4 * quarter)
        loads.append(pltpu.make_async_copy(coup_hbm.at[at4], coup.at[at4], in_sem.at[i]))
        loads.append(pltpu.make_async_copy(rhs_hbm.at[at], rhs.at[at], in_sem.at[4 + i]))
    loads.append(pltpu.make_async_copy(coup_rows_hbm, coup_rows, in_sem.at[8]))
    loads.append(pltpu.make_async_copy(rhs_rows_hbm, rhs_rows, in_sem.at[9]))
    weight_load = pltpu.make_async_copy(wv_hbm, w_v, in_sem.at[10])
    weight_load.start()
    for copy in loads[:8]:
        copy.start()
    loads.append(pltpu.make_async_copy(order_hbm, order, in_sem.at[11]))
    loads.append(pltpu.make_async_copy(w_hbm, w_s, in_sem.at[12]))

    barrier = pltpu.get_barrier_semaphore()
    everyone = plane_ids + [core_id] + z_ids
    for d in everyone:
        pl.semaphore_signal(barrier, inc=1, device_id=d, device_id_type=MESH)

    def send(src, dst, sems, i, d):
        copy = pltpu.make_async_remote_copy(
            src_ref=src, dst_ref=dst, send_sem=sems.at[0, i], recv_sem=sems.at[1, i],
            device_id=d, device_id_type=MESH,
        )
        copy.start()
        return copy

    def wait(copies):
        for copy in copies:
            copy.wait()

    def scatter(src, dst, sems):
        return [send(src.at[q], dst.at[i], sems, i, d) for i, (q, d) in enumerate(zip(plane_q, plane_ids))]

    def gather(src, dst, sems):
        return [send(src, dst.at[me], sems, i, d) for i, d in enumerate(plane_ids)]

    weight_load.wait()
    weight_cols = jnp.concatenate([w_v[...], jnp.zeros((112, 128), F32)], axis=0).T
    for g in range(16):
        if g % 4 == 0:
            wait(loads[g // 2 : g // 2 + 2])
        r0 = 128 * g
        col = jnp.broadcast_to(weight_cols[:, g : g + 1], (128, 128))
        for k in range(4):
            j = 3 - k
            basis = coup[pl.ds(4 * r0 + k, 128, stride=4), :]
            h, l = split(basis)
            xh[r0 : r0 + 128, 128 * j : 128 * j + 128] = h
            xl[r0 : r0 + 128, 128 * j : 128 * j + 128] = l
            h, l = split(basis * col)
            wh[r0 : r0 + 128, 128 * j : 128 * j + 128] = h
            wl[r0 : r0 + 128, 128 * j : 128 * j + 128] = l
        h, l = split(rhs[r0 : r0 + 128, :])
        xh[r0 : r0 + 128, 512:640] = h
        xl[r0 : r0 + 128, 512:640] = l

    for copy in loads[8:]:
        copy.start()

    def gram(a0, a1, b0, b1):
        return dot3(
            (wh[:, a0:a1], wl[:, a0:a1]), (xh[:, b0:b1], xl[:, b0:b1]), ((0,), (0,))
        )

    def pieces(value):
        return value.reshape(16, 8, 128)

    def put(ref, first, value):
        for k in range(value.shape[1] // 128):
            ref[:, first + k] = pieces(value[:, 128 * k : 128 * k + 128])

    put(ga, 0, gram(0, 128, 0, 256))
    pl.semaphore_wait(barrier, len(everyone))
    core_a = send(ga, ra, core_sem, 0, core_id)
    put(gb, 0, gram(0, 128, 256, 640))
    core_a.wait()
    ga[...] = ga[...] + ra[...]
    rs_a = scatter(ga, rsa, rsa_sem)
    put(gb, 3, gram(128, 256, 128, 256))
    core_b = send(gb, rb, core_sem, 1, core_id)
    m = gram(128, 256, 256, 640)
    for k in range(3):
        gc[0, :, k] = pieces(m[:, 128 * k : 128 * k + 128])
    core_b.wait()
    gb[...] = gb[...] + rb[...]
    rs_b = scatter(gb, rsb, rsb_sem)
    m = gram(256, 384, 256, 640)
    gc[0, :, 3] = pieces(m[:, :128])
    gc[1, :, 0] = pieces(m[:, 128:256])
    gc[1, :, 1] = pieces(m[:, 256:])
    m = gram(384, 512, 384, 640)
    gc[1, :, 2] = pieces(m[:, :128])
    gc[1, :, 3] = pieces(m[:, 128:])
    core_c = send(gc.at[1 - c], rc, core_sem, 2, core_id)
    wait(rs_a)
    pa[...] = ga[me] + jnp.sum(rsa[...], axis=0)
    fa[me] = pa[...]
    ag_a = gather(pa, fa, aga_sem)
    core_c.wait()
    rc[...] = rc[...] + gc[c]
    rs_c = scatter(rc, rsc, rsc_sem)
    wait(rs_b)
    pb[...] = gb[me] + jnp.sum(rsb[...], axis=0)
    fb[me] = pb[...]
    ag_b = gather(pb, fb, agb_sem)

    wait(loads[8:])

    def permute(t, carry):
        for u in range(8):
            i = t * 8 + u
            r = order[i]
            s = w_s[r]
            applied[pl.ds(pl.multiple_of(4 * i, 4), 4), :] = coup_rows[r] * s
            answer[pl.ds(i, 1), :] = rhs_rows[r] * s
        return carry

    lax.fori_loop(0, EARLY // 8, permute, 0)

    eye = jnp.where(
        lax.broadcasted_iota(jnp.int32, (128, 128), 0)
        == lax.broadcasted_iota(jnp.int32, (128, 128), 1),
        1.0,
        0.0,
    )

    def block(ref, k):
        return ref[:, k].reshape(128, 128)

    def blocks(ref, first, count):
        return jnp.concatenate([block(ref, first + k) for k in range(count)], axis=1)

    def inverse_of(lead, nodes):
        scale = nodes / AGENTS
        return invert(eye + lead * scale) * scale

    def offset(level):
        return sum(128 * (k + 1) for k in range(3, level, -1))

    def keep(level, p):
        h, l = split(p)
        ph[:, offset(level) : offset(level) + p.shape[1]] = h
        plo[:, offset(level) : offset(level) + p.shape[1]] = l

    def subtract(level, start=0, end=ROWS // CHUNK):
        cut = slice(offset(level), offset(level) + 128 * (level + 1))

        def body(t, carry):
            r0 = pl.multiple_of(t * CHUNK, CHUNK)
            lead = split(applied[pl.ds(4 * r0 + level, CHUNK, stride=4), :])
            change = dot3(lead, (ph[:, cut], plo[:, cut]))
            for k in range(level):
                at = pl.ds(4 * r0 + level - 1 - k, CHUNK, stride=4)
                applied[at, :] = applied[at, :] - change[:, 128 * k : 128 * k + 128]
            at = pl.ds(r0, CHUNK)
            answer[at, :] = answer[at, :] - change[:, 128 * level :]
            return carry

        lax.fori_loop(start, end, body, 0)

    def turn(ref, first, count):
        for k in range(count):
            mt[128 * k : 128 * k + 128, :] = block(ref, first + k).T

    def reduced(inverse, count, lead, rest):
        own = [mt[pl.ds(pl.multiple_of(128 * k + 8 * me, 8), 8), :] for k in range(count)]
        left = dot_full(jnp.concatenate([mt[0:128, :]] + own, axis=0), inverse)
        return dot_full(left[:128], lead), dot_full(left[128:], rest)

    wait(ag_a)
    turn(fa, 1, 1)
    wait(rs_c)
    pc[c] = rc[me] + jnp.sum(rsc[...], axis=0)
    core_p = send(pc.at[c], pc.at[c], core_sem, 3, core_id)
    inverse = inverse_of(block(fa, 0), 8.0)
    wait(ag_b)
    for k in range(2):
        mt[128 * k + 128 : 128 * k + 256, :] = block(fb, k).T
    m32 = block(fa, 1)
    rest = blocks(fb, 0, 3)
    full, part = reduced(inverse, 3, m32, rest)
    core_p.wait()
    where = [(0, 0), (0, 1), (0, 2), (1, 0), (1, 1), (1, 2), (2, 1), (2, 2)]
    for k, (i, j) in enumerate(where):
        z1ps[k] = pc[k // 4, k % 4] - part[8 * i : 8 * i + 8, 128 * j : 128 * j + 128]
    z1p = send(z1ps, z1pr, z_sem, 1, z_ids[0])
    z1s[...] = block(fb, 3) - full
    z1 = send(z1s, z1r, z_sem, 0, z_ids[0])
    keep(3, dot_full(inverse, jnp.concatenate([m32, rest], axis=1)))
    lax.fori_loop(EARLY // 8, ROWS // 8, permute, 0)
    z1p.wait()
    p2[...] = z1ps[...] + z1pr[...]
    fc[me] = p2[0:4]
    ag_c = gather(p2.at[0:4], fc, agc_sem)

    z1.wait()
    inverse = inverse_of(z1s[...] + z1r[...], 4.0)
    subtract(3, 0, LATER)
    wait(ag_c)
    turn(fc, 0, 2)
    m21 = block(fc, 0)
    rest = blocks(fc, 1, 2)
    full, part = reduced(inverse, 2, m21, rest)
    for k, (i, j) in enumerate([(0, 0), (0, 1), (1, 0), (1, 1)]):
        z2ps[k] = p2[4 + k] - part[8 * i : 8 * i + 8, 128 * j : 128 * j + 128]
    z2p = send(z2ps, z2pr, z_sem, 3, z_ids[1])
    z2s[...] = block(fc, 3) - full
    z2 = send(z2s, z2r, z_sem, 2, z_ids[1])
    keep(2, dot_full(inverse, jnp.concatenate([m21, rest], axis=1)))
    subtract(3, LATER)
    subtract(2, 0, 3)
    z2p.wait()
    p1[...] = z2ps[...] + z2pr[...]
    fd[me] = p1[...]
    ag_d = gather(p1, fd, agd_sem)

    z2.wait()
    inverse = inverse_of(z2s[...] + z2r[...], 2.0)
    subtract(2, 3)
    wait(ag_d)
    turn(fd, 0, 1)
    m1 = blocks(fd, 0, 2)
    left = dot_full(mt[0:128, :], inverse)
    z4s[...] = block(fd, 2) - dot_full(left, m1[:, :128])
    z4 = send(z4s, z4r, z_sem, 4, z_ids[2])
    z4bs[...] = block(fd, 3) - dot_full(left, m1[:, 128:])
    z4b = send(z4bs, z4br, z_sem, 5, z_ids[2])
    keep(1, dot_full(inverse, m1))
    subtract(1)
    h, l = split(applied[pl.ds(0, ROWS, stride=4), :])
    lead[:, :128] = h
    lead[:, 128:] = l
    outs = [
        pltpu.make_async_copy(a, b, out_sem.at[i])
        for i, (a, b) in enumerate(
            [(applied, applied_out), (answer, answer_out), (lead, lead_out)]
        )
    ]
    for copy in outs:
        copy.start()

    z4.wait()
    inverse = inverse_of(z4s[...] + z4r[...], 1.0)
    z4b.wait()
    h, l = split(dot_full(inverse, z4bs[...] + z4br[...]))
    p0[:128, :128] = h
    p0[:128, 128:] = l
    p0[128:, :128] = h
    p0[128:, 128:] = jnp.zeros((128, 128), BF)
    wait(outs)


PARTS = 8


def finish_kernel(applied_in, answer_in, lead, p0, applied_out, answer_out, ans, sem):
    rows = ROWS // PARTS
    outs = []
    for i in range(PARTS):
        at4 = pl.ds(4 * rows * i, 4 * rows)
        outs.append(pltpu.make_async_copy(applied_in.at[at4], applied_out.at[at4], sem.at[0, i]))
        outs[-1].start()
    for i in range(PARTS):
        at = pl.ds(rows * i, rows)
        change = jnp.dot(lead[at, :], p0[...], preferred_element_type=F32)
        ans[at, :] = answer_in[at, :] - (change[:, :128] + change[:, 128:])
        outs.append(pltpu.make_async_copy(ans.at[at], answer_out.at[at], sem.at[1, i]))
        outs[-1].start()
    for copy in outs:
        copy.wait()


def local(coupling, weights, rhs, order):
    def vmem(*shape, dtype=F32):
        return pltpu.VMEM(shape, dtype)

    def sems(n):
        return pltpu.SemaphoreType.DMA((2, n))

    whole = pl.BlockSpec(memory_space=pltpu.VMEM)
    anywhere = pl.BlockSpec(memory_space=pl.ANY)
    results = [
        jax.ShapeDtypeStruct((4 * ROWS, CAP), F32),
        jax.ShapeDtypeStruct((ROWS, CAP), F32),
    ]
    last = [jax.ShapeDtypeStruct((ROWS, 2 * CAP), BF), jax.ShapeDtypeStruct((2 * CAP, 2 * CAP), BF)]

    def in_hbm(v):
        return pltpu.with_memory_space_constraint(v, pltpu.HBM)

    state = pl.pallas_call(
        kernel,
        in_specs=[anywhere] * 7,
        out_specs=[anywhere] * 3 + [whole],
        out_shape=results + last,
        scratch_shapes=[
            pltpu.SMEM((ROWS,), jnp.int32), pltpu.SMEM((ROWS,), F32), vmem(16, CAP),
            vmem(4 * ROWS, CAP), vmem(ROWS, 4, CAP), vmem(ROWS, CAP), vmem(ROWS, 1, CAP),
            pltpu.SemaphoreType.DMA((13,)),
            vmem(4 * ROWS, CAP), vmem(ROWS, CAP), vmem(ROWS, 2 * CAP, dtype=BF),
            pltpu.SemaphoreType.DMA((3,)),
            vmem(ROWS, 640, dtype=BF), vmem(ROWS, 640, dtype=BF),
            vmem(ROWS, 512, dtype=BF), vmem(ROWS, 512, dtype=BF),
            vmem(16, 2, 8, 128), vmem(16, 2, 8, 128), vmem(15, 2, 8, 128), vmem(2, 8, 128), vmem(16, 2, 8, 128),
            vmem(16, 4, 8, 128), vmem(16, 4, 8, 128), vmem(15, 4, 8, 128), vmem(4, 8, 128), vmem(16, 4, 8, 128),
            vmem(2, 16, 4, 8, 128), vmem(16, 4, 8, 128), vmem(15, 4, 8, 128), vmem(2, 4, 8, 128),
            vmem(16, 4, 8, 128), vmem(16, 4, 8, 128),
            vmem(128, 128), vmem(128, 128), vmem(8, 8, 128), vmem(8, 8, 128), vmem(8, 8, 128),
            vmem(128, 128), vmem(128, 128), vmem(4, 8, 128), vmem(4, 8, 128), vmem(4, 8, 128),
            vmem(128, 128), vmem(128, 128), vmem(128, 128), vmem(128, 128),
            vmem(128, 1280, dtype=BF), vmem(128, 1280, dtype=BF), vmem(384, 128),
            sems(4), sems(15), sems(15), sems(15), sems(15), sems(15), sems(15), sems(15), sems(6),
        ],
        compiler_params=pltpu.CompilerParams(
            collective_id=0, has_side_effects=True, vmem_limit_bytes=44 * 2**20
        ),
        name="hodlr",
    )(
        in_hbm(order.reshape(ROWS)),
        in_hbm(weights),
        in_hbm(weights.reshape(ROWS // 128, 128)),
        in_hbm(coupling.reshape(4 * ROWS, CAP)),
        in_hbm(coupling),
        in_hbm(rhs),
        in_hbm(rhs.reshape(ROWS, 1, CAP)),
    )
    applied, answer = pl.pallas_call(
        finish_kernel,
        in_specs=[anywhere] + [whole] * 3,
        out_specs=[anywhere, anywhere],
        out_shape=results,
        scratch_shapes=[vmem(ROWS, CAP), sems(PARTS)],
        compiler_params=pltpu.CompilerParams(vmem_limit_bytes=16 * 2**20),
        name="finish",
    )(*state)
    return applied.reshape(ROWS, 4, CAP), answer


def solution(mesh):
    rows = ("leaf", "sub")
    return jax.shard_map(
        local,
        mesh=mesh,
        in_specs=(P(rows, None, None), P(rows), P(rows, None), P(rows, None)),
        out_specs=(P(rows, None, None), P(rows, None)),
        check_vma=False,
    )
```
